32 devices in a mesh: dp: 4 (over y, x), seq: 8 (over z, core).
Axes of the slice: x: 2, y: 2, z: 4, core: 2. Of those that a mesh axis runs over, the one named last changes fastest.
Arguments:
- tokens: bfloat16 [64, 1024, 768], P(('dp', 'seq')), may hold values from -6 to 6
- lengths: int32 [64], P(('dp', 'seq')), may hold values from 64 to 1024, as said below
- mixer: bfloat16 [12, 1024, 1024], P('dp', 'seq'), may hold values from -8 to 8
- gain_one: bfloat16 [768], P(('dp', 'seq')), may hold values from 0.099609375 to 1.8984375
- gain_two: bfloat16 [768], P(('dp', 'seq')), may hold values from 0.099609375 to 1.8984375
- w_value: bfloat16 [768, 768], P(('dp', 'seq')), may hold values from -0.21875 to 0.21875
- w_out: bfloat16 [768, 768], P(('dp', 'seq')), may hold values from -1.75 to 1.75
- w_up: bfloat16 [768, 3072], P(('dp', 'seq')), may hold values from -0.21875 to 0.21875
- w_down: bfloat16 [3072, 768], P(('dp', 'seq')), may hold values from -0.15625 to 0.15625
- cotangent: bfloat16 [64, 1024, 768], P(('dp', 'seq')), may hold values from -6 to 6
Outputs:
- output: bfloat16 [64, 1024, 768], P(('dp', 'seq'))
- grad_tokens: bfloat16 [64, 1024, 768], P(('dp', 'seq'))
- grad_mixer: float32 [12, 1024, 1024], P('dp', 'seq')
- grad_gain_one: float32 [768], P(('dp', 'seq'))
- grad_gain_two: float32 [768], P(('dp', 'seq'))
- grad_w_value: float32 [768, 768], P(('dp', 'seq'))
- grad_w_out: float32 [768, 768], P(('dp', 'seq'))
- grad_w_up: float32 [768, 3072], P(('dp', 'seq'))
- grad_w_down: float32 [3072, 768], P(('dp', 'seq'))
The draws below stay inside these ranges and needn't reach their ends.
Inputs may be any that keep to these rules, and one draw needn't show every extreme that they name: `lengths`: valid prefix of each item; in every draw some item has length 1024 and some item 64.
All inputs are finite; a program needn't handle non-finite values.
Results may differ from the reference program's by a relative error of at most 0.017.
Values may be sent and summed in bfloat16 or wider, within the bound.
No kernel may reach another device: no remote copies, remote signals or barrier semaphores. Data moves between devices by JAX's collectives and lax.ppermute only.
A program may use at most 448 MiB of HBM per device.

```python
import jax
import jax.numpy as jnp
from jax import lax

HEADS = 12
HEAD_DIM = 64
FF = 3072
LEN = 1024
MIN_LEN = 64
D = 768
ITEMS = 64


def draw_lengths(key, part):
    key = jax.random.fold_in(key, 11)
    key_draw, key_full, key_short = jax.random.split(key, 3)
    values = jax.random.randint(key_draw, (ITEMS,), MIN_LEN, LEN + 1, dtype=jnp.int32)
    full_at = jax.random.randint(key_full, (), 0, ITEMS, dtype=jnp.int32)
    short_at = (full_at + 1 + jax.random.randint(key_short, (), 0, ITEMS - 1, dtype=jnp.int32)) % ITEMS
    positions = jnp.arange(ITEMS, dtype=jnp.int32)
    values = jnp.where(positions == full_at, LEN, values)
    values = jnp.where(positions == short_at, MIN_LEN, values)
    return values.astype(jnp.int32)


def block_scale(stream_key, dims, pieces, low, high):
    loudness, own = 1.0, jax.random.fold_in(stream_key, 6)
    for axis_at, shards_of in pieces:
        steps = jnp.exp(jax.random.uniform(jax.random.fold_in(own, axis_at), (shards_of,), jnp.float32, low / len(pieces), high / len(pieces)))
        loudness = loudness * jnp.repeat(steps, dims[axis_at] // shards_of).reshape([-1 if axis == axis_at else 1 for axis in range(len(dims))])
    return loudness


def bell_draw(key, dims, width, bound, cuts=(), held_as=jnp.bfloat16):
    array = jax.random.normal(key, dims, jnp.float32) * width
    if len(cuts) > 0:
        array = block_scale(key, dims, cuts, -0.22, 0.18) * array
    return jnp.clip(array, min=-bound, max=bound).astype(held_as)


def setup_inputs(seed: int = 0) -> dict:
    splits = jax.random.split(jax.random.key(seed), 11)
    return {
        "tokens": bell_draw(splits[0], (ITEMS, LEN, D), 1.0, 6.0, ((0, 32),)),
        "lengths": draw_lengths(jax.random.fold_in(splits[10], 71), 0),
        "mixer": bell_draw(splits[2], (HEADS, LEN, LEN), 1.5, 8.0, ((0, 4), (1, 8))),
        "gain_one": jnp.clip(1.0 + 0.18 * jax.random.normal(splits[3], (D,), jnp.float32), 0.099609375, 1.8984375).astype(jnp.bfloat16),
        "gain_two": jnp.clip(1.0 + 0.18 * jax.random.normal(splits[4], (D,), jnp.float32), 0.099609375, 1.8984375).astype(jnp.bfloat16),
        "w_value": bell_draw(splits[5], (D, D), D ** -0.5, 0.21875, ((0, 32),)),
        "w_out": bell_draw(splits[6], (D, D), (max(D * 16 // LEN, 1)) ** -0.5, 1.75, ((0, 32),)),
        "w_up": bell_draw(splits[7], (D, FF), D ** -0.5, 0.21875, ((0, 32),)),
        "w_down": bell_draw(splits[8], (FF, D), (FF // 2) ** -0.5, 0.15625, ((0, 32),)),
        "cotangent": bell_draw(splits[9], (ITEMS, LEN, D), 1.0, 6.0, ((0, 32),)),
    }


@jax.custom_vjp
def low(v):
    return lax.optimization_barrier(v.astype(jnp.bfloat16)).astype(jnp.float32)

@jax.custom_vjp
def low_back(v):
    return v

def low_keep(v):
    return (low(v), None)

def low_pass(kept, grad):
    return (grad,)

def back_keep(v):
    return (v, None)

def back_low(kept, grad):
    return (low(grad),)
low.defvjp(low_keep, low_pass)
low_back.defvjp(back_keep, back_low)
epsilon = 1e-06

def matmul(left, right):
    return jnp.dot(left, right, precision=lax.Precision.HIGHEST)

def rms_scale(inputs, gain):
    return inputs * lax.rsqrt(lax.optimization_barrier(jnp.mean(inputs * inputs, axis=-1, keepdims=True)) + epsilon) * gain

def mixing(mixer, values, length):
    positions = jnp.arange(LEN, dtype=jnp.int32)
    keep_keys = positions[None, None, :] < length
    masked = jnp.where(keep_keys, mixer, -1e+30)
    top = lax.optimization_barrier(jnp.max(masked, axis=-1, keepdims=True))
    expos = jnp.where(keep_keys, jnp.exp(masked - top), 0.0)
    probs = expos / lax.optimization_barrier(jnp.sum(expos, axis=-1, keepdims=True))
    probs = jnp.where(positions[None, :, None] < length, probs, 0.0)
    probs = low(probs)
    split = values.reshape(LEN, HEADS, HEAD_DIM)
    mixed = jnp.einsum('hij,jhd->ihd', probs, split, precision=lax.Precision.HIGHEST)
    return mixed.reshape(LEN, HEADS * HEAD_DIM)

def layer_item(inputs, length, mixer, gain_one, gain_two, w_value, w_out, w_up, w_down):
    normed = low(rms_scale(inputs, gain_one))
    values = low(low_back(matmul(normed, w_value)))
    mixed = low(low_back(mixing(mixer, values, length)))
    hidden = inputs + low_back(matmul(mixed, w_out))
    normed_two = low(rms_scale(hidden, gain_two))
    active = low(jax.nn.gelu(low_back(matmul(normed_two, w_up)), approximate=True))
    return hidden + matmul(active, w_down)

def reference(tokens, lengths, mixer, gain_one, gain_two, w_value, w_out, w_up, w_down, cotangent):
    params = tuple((weight.astype(jnp.float32) for weight in (mixer, gain_one, gain_two, w_value, w_out, w_up, w_down)))
    inputs = tokens.astype(jnp.float32)
    checked = jax.checkpoint(layer_item)

    def forward(inputs, params):

        def step(carry, entry):
            return (carry, checked(entry[0], entry[1], *params))
        _, result = lax.scan(step, None, (inputs, lengths))
        return result
    result, pullback = jax.vjp(forward, inputs, params)
    grad_inputs, grad_params = pullback(cotangent.astype(jnp.float32))
    return (result.astype(jnp.bfloat16), grad_inputs.astype(jnp.bfloat16), grad_params[0], grad_params[1], grad_params[2], grad_params[3], grad_params[4], grad_params[5], grad_params[6])
```

```python
import functools

import jax
import jax.numpy as jnp
from jax import lax
from jax.experimental import pallas as pl
from jax.experimental.pallas import tpu as pltpu
from jax.sharding import PartitionSpec as P

epsilon = 1e-06
bf16 = jnp.bfloat16
f32 = jnp.float32
WIDTH = 768
LENGTH = 1024
HIDDEN = 3072
HEADS = 12
HEAD_DIM = 64
CHUNKS = 4
VMEM = 58 * 1024 * 1024


def rows_by_rows(left, right):
    return lax.dot_general(left, right, (((1,), (1,)), ((), ())), preferred_element_type=f32)


def times(left, right):
    return jnp.dot(left, right, preferred_element_type=f32)


def rms(values):
    return lax.rsqrt(jnp.mean(values * values, axis=-1, keepdims=True) + epsilon)


def params(**more):
    return pltpu.CompilerParams(vmem_limit_bytes=VMEM, **more)


def cost(flops, moved):
    return pl.CostEstimate(flops=int(flops), bytes_accessed=int(moved), transcendentals=0)


def spread(scratch, refs, place, group):
    for at, ref in enumerate(refs):
        start = pl.multiple_of((place ^ at) * group, 64)
        scratch[pl.ds(start, group), :] = ref[0]


def pick(scratch, refs, place, group):
    for at, ref in enumerate(refs):
        start = pl.multiple_of((place ^ at) * group, 64)
        ref[0] = scratch[pl.ds(start, group), :]


def values_kernel(where, x_ref, w_ref, *rest):
    outs, (turned, scratch) = rest[:-2], rest[-2:]

    @pl.when((pl.program_id(0) == 0) & (pl.program_id(1) == 0))
    def _():
        turned[...] = w_ref[...].T

    x = x_ref[0].astype(f32)
    scaled = (x * rms(x)).astype(bf16)
    scratch[...] = rows_by_rows(turned[...], scaled).astype(bf16)
    pick(scratch, outs, where[0], outs[0].shape[1])


def project_values(where, tokens, weight, groups):
    items = tokens.shape[0]
    rows = 512
    group = WIDTH // groups
    return pl.pallas_call(
        values_kernel,
        grid_spec=pltpu.PrefetchScalarGridSpec(
            num_scalar_prefetch=1,
            grid=(items, LENGTH // rows),
            in_specs=[
                pl.BlockSpec((1, rows, WIDTH), lambda i, j, s: (i, j, 0)),
                pl.BlockSpec((WIDTH, WIDTH), lambda i, j, s: (0, 0)),
            ],
            out_specs=[pl.BlockSpec((1, group, rows), lambda i, j, s: (i, 0, j))] * groups,
            scratch_shapes=[pltpu.VMEM((WIDTH, WIDTH), bf16), pltpu.VMEM((WIDTH, rows), bf16)],
        ),
        out_shape=[jax.ShapeDtypeStruct((items, group, LENGTH), bf16)] * groups,
        compiler_params=params(),
        cost_estimate=cost(2 * items * LENGTH * WIDTH * WIDTH, 4 * items * LENGTH * WIDTH),
        name="project_values",
    )(where, tokens, weight)


def load_logits(offsets, pieces, held, sems, first):
    def copy(head, at):
        rows = pieces[at].shape[1]
        start = pl.multiple_of(offsets[at], rows)
        return pltpu.make_async_copy(
            pieces[at].at[head], held.at[head, pl.ds(start, rows)], sems.at[head, at]
        )

    head = pl.program_id(0)

    @pl.when(first)
    def _():
        for h in range(held.shape[0]):
            for at in range(len(pieces)):
                copy(h, at).start()

    for at in range(len(pieces)):
        copy(head, at).wait()


def mix_kernel(lengths, offsets, *rest, groups, pieces):
    values, parts = rest[:groups], rest[groups : groups + pieces]
    outs = rest[groups + pieces : 2 * groups + pieces]
    sums_ref, held, left, sems = rest[2 * groups + pieces :]
    load_logits(offsets, parts, held, sems, pl.program_id(0) == 0)
    items = values[0].shape[0]
    total = groups * items
    places = lax.broadcasted_iota(jnp.int32, (1, LENGTH), 1)
    for k in range(total):
        block = values[k // items][k % items]
        keep = places < lengths[k]
        left[pl.ds(k * HEAD_DIM, HEAD_DIM), :] = jnp.where(keep, block, jnp.zeros_like(block))
    which = lax.broadcasted_iota(jnp.int32, (16, LENGTH), 0)
    reach = jnp.zeros((16, LENGTH), jnp.int32)
    for k in range(total):
        reach = jnp.where(which == k, lengths[k], reach)
    columns = lax.broadcasted_iota(jnp.int32, (16, LENGTH), 1)
    left[pl.ds(total * HEAD_DIM, 16), :] = jnp.where(columns < reach, 1.0, 0.0).astype(bf16)
    product = rows_by_rows(left[...], held[pl.program_id(0)])
    sums = product[total * HEAD_DIM : total * HEAD_DIM + total]
    sums_ref[0] = sums
    for k in range(total):
        mixed = product[k * HEAD_DIM : (k + 1) * HEAD_DIM] / sums[k : k + 1]
        keep = places < lengths[k]
        outs[k // items][k % items] = jnp.where(keep, mixed, 0.0).astype(bf16)


def mix_items(lengths, offsets, values, parts):
    groups, pieces = len(values), len(parts)
    items, group, _ = values[0].shape
    heads = group // HEAD_DIM
    total = groups * items
    block = pl.BlockSpec((items, HEAD_DIM, LENGTH), lambda h, s, o: (0, h, 0))
    outs = pl.pallas_call(
        functools.partial(mix_kernel, groups=groups, pieces=pieces),
        grid_spec=pltpu.PrefetchScalarGridSpec(
            num_scalar_prefetch=2,
            grid=(heads,),
            in_specs=[block] * groups + [pl.BlockSpec(memory_space=pl.ANY)] * pieces,
            out_specs=[block] * groups
            + [pl.BlockSpec((1, total, LENGTH), lambda h, s, o: (h, 0, 0))],
            scratch_shapes=[
                pltpu.VMEM((heads, LENGTH, LENGTH), bf16),
                pltpu.VMEM((total * HEAD_DIM + 16, LENGTH), bf16),
                pltpu.SemaphoreType.DMA((heads, pieces)),
            ],
        ),
        out_shape=[jax.ShapeDtypeStruct((items, group, LENGTH), bf16)] * groups
        + [jax.ShapeDtypeStruct((heads, total, LENGTH), f32)],
        compiler_params=params(),
        cost_estimate=cost(2 * heads * total * 66 * LENGTH * LENGTH, 12 << 20),
        name="mix_items",
    )(lengths, offsets, *values, *parts)
    return outs[:groups], outs[groups]


def mix_back_kernel(lengths, offsets, *rest, groups, pieces, shares):
    grads, values, mixed = (rest[k * groups : (k + 1) * groups] for k in range(3))
    rest = rest[3 * groups :]
    sums_ref, parts = rest[0], rest[1 : 1 + pieces]
    outs = rest[1 + pieces : 1 + pieces + groups]
    rest = rest[1 + pieces + groups :]
    shares_refs = rest[: len(shares)]
    held, left, right, whole, sems = rest[len(shares) :]
    load_logits(offsets, parts, held, sems, pl.program_id(0) == 0)
    items = values[0].shape[0]
    total = groups * items
    places = lax.broadcasted_iota(jnp.int32, (1, LENGTH), 1)
    which = lax.broadcasted_iota(jnp.int32, (16, LENGTH), 0)
    base = total * HEAD_DIM
    extra_left = jnp.zeros((16, LENGTH), f32)
    extra_right = jnp.zeros((16, LENGTH), f32)
    for k in range(total):
        keep = places < lengths[k]
        inverse = jnp.where(keep, 1.0 / sums_ref[0, k : k + 1], 0.0)
        grad = grads[k // items][k % items].astype(f32)
        delta = jnp.sum(grad * mixed[k // items][k % items].astype(f32), axis=0, keepdims=True)
        left[pl.ds(k * HEAD_DIM, HEAD_DIM), :] = (grad * inverse).astype(bf16)
        extra_left = jnp.where(which == k, -(delta * inverse), extra_left)
        extra_right = jnp.where((which == k) & keep, 1.0, extra_right)
        block = values[k // items][k % items]
        right[pl.ds(k * HEAD_DIM, HEAD_DIM), :] = jnp.where(keep, block, jnp.zeros_like(block))
    left[pl.ds(base, 16), :] = extra_left.astype(bf16)
    right[pl.ds(base, 16), :] = extra_right.astype(bf16)
    grad_values = times(left[pl.ds(0, base), :], held[pl.program_id(0)])
    for k in range(total):
        keep = places < lengths[k]
        part = grad_values[k * HEAD_DIM : (k + 1) * HEAD_DIM]
        outs[k // items][k % items] = jnp.where(keep, part, 0.0).astype(bf16)
    whole[...] = times(left[...].T, right[...]).astype(bf16)
    at = pieces
    for ref, (count, rows) in zip(shares_refs, shares):
        for k in range(count):
            ref[k, 0] = whole[pl.ds(pl.multiple_of(offsets[at], rows), rows), :]
            at += 1


def mix_back(lengths, offsets, grads, values, mixed, sums, parts, shares):
    groups, pieces = len(values), len(parts)
    items, group, _ = values[0].shape
    heads = group // HEAD_DIM
    total = groups * items
    block = pl.BlockSpec((items, HEAD_DIM, LENGTH), lambda h, s, o: (0, h, 0))
    outs = pl.pallas_call(
        functools.partial(mix_back_kernel, groups=groups, pieces=pieces, shares=shares),
        grid_spec=pltpu.PrefetchScalarGridSpec(
            num_scalar_prefetch=2,
            grid=(heads,),
            in_specs=[block] * (3 * groups)
            + [pl.BlockSpec((1, total, LENGTH), lambda h, s, o: (h, 0, 0))]
            + [pl.BlockSpec(memory_space=pl.ANY)] * pieces,
            out_specs=[block] * groups
            + [
                pl.BlockSpec((count, 1, rows, LENGTH), lambda h, s, o: (0, h, 0, 0))
                for count, rows in shares
            ],
            scratch_shapes=[
                pltpu.VMEM((heads, LENGTH, LENGTH), bf16),
                pltpu.VMEM((total * HEAD_DIM + 16, LENGTH), bf16),
                pltpu.VMEM((total * HEAD_DIM + 16, LENGTH), bf16),
                pltpu.VMEM((LENGTH, LENGTH), bf16),
                pltpu.SemaphoreType.DMA((heads, pieces)),
            ],
        ),
        out_shape=[jax.ShapeDtypeStruct((items, group, LENGTH), bf16)] * groups
        + [jax.ShapeDtypeStruct((count, heads, rows, LENGTH), bf16) for count, rows in shares],
        compiler_params=params(),
        cost_estimate=cost(4 * heads * total * 66 * LENGTH * LENGTH, 24 << 20),
        name="mix_back",
    )(lengths, offsets, *grads, *values, *mixed, sums, *parts)
    return outs[:groups], outs[groups:]


def attend_kernel(where, *rest, groups):
    mixed, (x_ref, w_ref, hidden_ref, scaled_ref, scratch) = rest[:groups], rest[groups:]
    spread(scratch, mixed, where[0], mixed[0].shape[1])
    hidden = x_ref[0].astype(f32) + times(scratch[...].T, w_ref[...])
    hidden_ref[0] = hidden
    scaled_ref[0] = (hidden * rms(hidden)).astype(bf16)


def attend(where, mixed, tokens, weight):
    groups = len(mixed)
    items, group, _ = mixed[0].shape
    rows = 512
    tall = pl.BlockSpec((1, rows, WIDTH), lambda i, j, s: (i, j, 0))
    return pl.pallas_call(
        functools.partial(attend_kernel, groups=groups),
        grid_spec=pltpu.PrefetchScalarGridSpec(
            num_scalar_prefetch=1,
            grid=(items, LENGTH // rows),
            in_specs=[pl.BlockSpec((1, group, rows), lambda i, j, s: (i, 0, j))] * groups
            + [tall, pl.BlockSpec((WIDTH, WIDTH), lambda i, j, s: (0, 0))],
            out_specs=[tall, tall],
            scratch_shapes=[pltpu.VMEM((WIDTH, rows), bf16)],
        ),
        out_shape=[
            jax.ShapeDtypeStruct(tokens.shape, f32),
            jax.ShapeDtypeStruct(tokens.shape, bf16),
        ],
        compiler_params=params(),
        cost_estimate=cost(2 * items * LENGTH * WIDTH * WIDTH, 16 << 20),
        name="attend",
    )(where, *mixed, tokens, weight)


FIRST = 0.7978845608028654
SECOND = FIRST * 0.044715


def feed_kernel(scaled_ref, grad_ref, up_ref, down_ref, *rest, carried):
    before, rest = rest[: 2 * carried], rest[2 * carried :]
    out_ref, back_ref, grad_up_ref, grad_down_ref = rest[:4]
    up_turned, down_turned, active, grad_pre, sum_up, sum_down = rest[4:]
    step = pl.program_id(0)
    units = down_ref.shape[0]

    @pl.when(step == 0)
    def _():
        up_turned[...] = up_ref[...].T
        down_turned[...] = down_ref[...].T

    scaled, grad = scaled_ref[...], grad_ref[...]
    slab = 256
    for k in range(units // slab):
        at = pl.ds(k * slab, slab)
        pre = rows_by_rows(up_turned[at, :], scaled)
        grad_active = rows_by_rows(down_ref[at, :], grad)
        square = pre * pre
        half = 0.5 + 0.5 * jnp.tanh(pre * (FIRST + SECOND * square))
        act = pre * half
        active[at, :] = act.astype(bf16)
        slope = half + act * (1.0 - half) * (2.0 * FIRST + 6.0 * SECOND * square)
        grad_pre[at, :] = (grad_active * slope).astype(bf16)
    out = times(down_turned[...], active[...])
    back = times(up_ref[...], grad_pre[...])
    if carried:
        out, back = out + before[0][...], back + before[1][...]
    out_ref[...] = out
    back_ref[...] = back
    down = times(active[...], grad)
    up = times(grad_pre[...], scaled)

    @pl.when(step == 0)
    def _():
        sum_down[...] = down
        sum_up[...] = up

    @pl.when(step > 0)
    def _():
        sum_down[...] += down
        sum_up[...] += up

    @pl.when(step == pl.num_programs(0) - 1)
    def _():
        grad_down_ref[...] = sum_down[...].astype(bf16)
        grad_up_ref[...] = sum_up[...].T.astype(bf16)


def feed(scaled, grad, up, down, before):
    rows = 512
    total = scaled.shape[0]
    units = down.shape[0]
    tall = pl.BlockSpec((rows, WIDTH), lambda j: (j, 0))
    wide = pl.BlockSpec((WIDTH, rows), lambda j: (0, j))
    up_block = pl.BlockSpec((WIDTH, units), lambda j: (0, 0))
    down_block = pl.BlockSpec((units, WIDTH), lambda j: (0, 0))
    return pl.pallas_call(
        functools.partial(feed_kernel, carried=bool(before)),
        grid=(total // rows,),
        in_specs=[tall, tall, up_block, down_block] + [wide] * len(before),
        out_specs=[wide, wide, up_block, down_block],
        scratch_shapes=[
            pltpu.VMEM((units, WIDTH), bf16),
            pltpu.VMEM((WIDTH, units), bf16),
            pltpu.VMEM((units, rows), bf16),
            pltpu.VMEM((units, rows), bf16),
            pltpu.VMEM((units, WIDTH), f32),
            pltpu.VMEM((units, WIDTH), f32),
        ],
        out_shape=[
            jax.ShapeDtypeStruct((WIDTH, total), f32),
            jax.ShapeDtypeStruct((WIDTH, total), f32),
            jax.ShapeDtypeStruct((WIDTH, units), bf16),
            jax.ShapeDtypeStruct((units, WIDTH), bf16),
        ],
        input_output_aliases={4: 0, 5: 1} if before else {},
        compiler_params=params(),
        cost_estimate=cost(12 * total * WIDTH * units, 30 << 20),
        name="feed",
    )(scaled, grad, up, down, *before)


def finish_kernel(where, out_ref, back_ref, hidden_ref, grad_ref, w_ref, *rest, groups):
    mixed, rest = rest[:groups], rest[groups:]
    result_ref, grad_hidden_ref = rest[:2]
    grads, rest = rest[2 : 2 + groups], rest[2 + groups :]
    grad_w_ref, gain_ref, scratch, turned, sum_w, sum_gain = rest
    first = (pl.program_id(0) == 0) & (pl.program_id(1) == 0)
    last = (pl.program_id(0) == pl.num_programs(0) - 1) & (
        pl.program_id(1) == pl.num_programs(1) - 1
    )
    hidden = hidden_ref[0]
    result_ref[0] = (hidden + out_ref[...].T).astype(bf16)
    weighted = back_ref[...].T
    scale = rms(hidden)
    both = weighted * hidden
    mean = jnp.mean(both, axis=-1, keepdims=True)
    grad_hidden = grad_ref[0].astype(f32) + scale * weighted - hidden * (scale**3 * mean)
    attended = grad_hidden.astype(bf16)
    grad_hidden_ref[0] = attended
    gain = jnp.sum(both * scale, axis=0, keepdims=True)
    group = mixed[0].shape[1]
    scratch[...] = rows_by_rows(w_ref[...], attended).astype(bf16)
    pick(scratch, grads, where[0], group)
    spread(turned, mixed, where[0], group)
    part = times(turned[...], attended)

    @pl.when(first)
    def _():
        sum_w[...] = part
        sum_gain[...] = gain

    @pl.when(jnp.logical_not(first))
    def _():
        sum_w[...] += part
        sum_gain[...] += gain

    @pl.when(last)
    def _():
        grad_w_ref[...] = sum_w[...].astype(bf16)
        gain_ref[...] = sum_gain[...]


def finish(where, out, back, hidden, grad, weight, mixed):
    groups = len(mixed)
    items, group, _ = mixed[0].shape
    rows = 512
    steps = LENGTH // rows
    tall = pl.BlockSpec((1, rows, WIDTH), lambda i, j, s: (i, j, 0))
    wide = pl.BlockSpec((WIDTH, rows), lambda i, j, s: (0, i * steps + j))
    square = pl.BlockSpec((WIDTH, WIDTH), lambda i, j, s: (0, 0))
    split = pl.BlockSpec((1, group, rows), lambda i, j, s: (i, 0, j))
    outs = pl.pallas_call(
        functools.partial(finish_kernel, groups=groups),
        grid_spec=pltpu.PrefetchScalarGridSpec(
            num_scalar_prefetch=1,
            grid=(items, steps),
            in_specs=[wide, wide, tall, tall, square] + [split] * groups,
            out_specs=[tall, tall]
            + [split] * groups
            + [square, pl.BlockSpec((1, WIDTH), lambda i, j, s: (0, 0))],
            scratch_shapes=[
                pltpu.VMEM((WIDTH, rows), bf16),
                pltpu.VMEM((WIDTH, rows), bf16),
                pltpu.VMEM((WIDTH, WIDTH), f32),
                pltpu.VMEM((1, WIDTH), f32),
            ],
        ),
        out_shape=[
            jax.ShapeDtypeStruct(grad.shape, bf16),
            jax.ShapeDtypeStruct(grad.shape, bf16),
        ]
        + [jax.ShapeDtypeStruct((items, group, LENGTH), bf16)] * groups
        + [
            jax.ShapeDtypeStruct((WIDTH, WIDTH), bf16),
            jax.ShapeDtypeStruct((1, WIDTH), f32),
        ],
        compiler_params=params(),
        cost_estimate=cost(4 * items * LENGTH * WIDTH * WIDTH, 34 << 20),
        name="finish",
    )(where, out, back, hidden, grad, weight, *mixed)
    return outs[0], outs[1], outs[2 : 2 + groups], outs[2 + groups], outs[3 + groups]


def tokens_kernel(where, x_ref, grad_ref, w_ref, *rest, groups):
    grads, rest = rest[:groups], rest[groups:]
    result_ref, grad_w_ref, gain_ref, turned, sum_w, sum_gain = rest
    first = (pl.program_id(0) == 0) & (pl.program_id(1) == 0)
    last = (pl.program_id(0) == pl.num_programs(0) - 1) & (
        pl.program_id(1) == pl.num_programs(1) - 1
    )
    spread(turned, grads, where[0], grads[0].shape[1])
    x = x_ref[0].astype(f32)
    scale = rms(x)
    scaled = (x * scale).astype(bf16)
    weighted = rows_by_rows(turned[...].T, w_ref[...])
    both = weighted * x
    mean = jnp.mean(both, axis=-1, keepdims=True)
    total = grad_ref[0].astype(f32) + scale * weighted - x * (scale**3 * mean)
    result_ref[0] = total.astype(bf16)
    gain = jnp.sum(both * scale, axis=0, keepdims=True)
    part = times(turned[...], scaled)

    @pl.when(first)
    def _():
        sum_w[...] = part
        sum_gain[...] = gain

    @pl.when(jnp.logical_not(first))
    def _():
        sum_w[...] += part
        sum_gain[...] += gain

    @pl.when(last)
    def _():
        grad_w_ref[...] = sum_w[...].T.astype(bf16)
        gain_ref[...] = sum_gain[...]


def grad_tokens_of(where, tokens, grad_hidden, weight, grads):
    groups = len(grads)
    items, group, _ = grads[0].shape
    rows = 512
    tall = pl.BlockSpec((1, rows, WIDTH), lambda i, j, s: (i, j, 0))
    square = pl.BlockSpec((WIDTH, WIDTH), lambda i, j, s: (0, 0))
    return pl.pallas_call(
        functools.partial(tokens_kernel, groups=groups),
        grid_spec=pltpu.PrefetchScalarGridSpec(
            num_scalar_prefetch=1,
            grid=(items, LENGTH // rows),
            in_specs=[tall, tall, square]
            + [pl.BlockSpec((1, group, rows), lambda i, j, s: (i, 0, j))] * groups,
            out_specs=[tall, square, pl.BlockSpec((1, WIDTH), lambda i, j, s: (0, 0))],
            scratch_shapes=[
                pltpu.VMEM((WIDTH, rows), bf16),
                pltpu.VMEM((WIDTH, WIDTH), f32),
                pltpu.VMEM((1, WIDTH), f32),
            ],
        ),
        out_shape=[
            jax.ShapeDtypeStruct(tokens.shape, bf16),
            jax.ShapeDtypeStruct((WIDTH, WIDTH), bf16),
            jax.ShapeDtypeStruct((1, WIDTH), f32),
        ],
        compiler_params=params(),
        cost_estimate=cost(4 * items * LENGTH * WIDTH * WIDTH, 14 << 20),
        name="grad_tokens",
    )(where, tokens, grad_hidden, weight, *grads)


ALL = ("dp", "seq")


def exchange(parts):
    got = [parts[0]]
    for r in range(1, len(parts)):
        got.append(lax.ppermute(parts[r], "dp", [(i, i ^ r) for i in range(len(parts))]))
    return got


def body(tokens, lengths, mixer, gain_one, gain_two, w_value, w_out, w_up, w_down, cotangent, groups, seqs):
    ranks = groups * seqs
    here, row = lax.axis_index("dp"), lax.axis_index("seq")
    where = jnp.stack([here, row]).astype(jnp.int32)
    items = tokens.shape[0]
    shard = w_value.shape[0]
    slices = HIDDEN // WIDTH

    first_gain = gain_one.astype(f32)[:, None]
    second_gain = gain_two.astype(f32)[:, None]
    value_mine = (w_value.astype(f32) * first_gain).astype(bf16)
    up_mine = (w_up.astype(f32) * second_gain).astype(bf16)

    value_all = lax.all_gather(value_mine, ALL, axis=0, tiled=True)
    packed = jnp.concatenate([w_out, up_mine.reshape(shard * slices, WIDTH), w_down], axis=0)
    gathered = lax.all_gather(packed, ALL, axis=0, tiled=False)
    out_all = gathered[:, :shard].reshape(WIDTH, WIDTH)
    up_all = jnp.moveaxis(
        gathered[:, shard : shard * (1 + slices)].reshape(WIDTH, slices, WIDTH), 1, 0
    )
    down_all = gathered[:, shard * (1 + slices) :].reshape(slices, WIDTH, WIDTH)

    logits = jnp.exp(mixer.astype(f32))
    logits_low = logits.astype(bf16)
    logits_parts = [lax.all_gather(logits_low, "seq", axis=1, tiled=True)]
    shares = ((1, LENGTH),)
    offsets = jnp.zeros((2,), jnp.int32)

    lengths_here = jnp.concatenate(exchange([lengths] * groups))
    values = exchange(project_values(where, tokens, value_all, groups))
    mixed_out, sums = mix_items(lengths_here, offsets, values, logits_parts)
    mixed = exchange(mixed_out)
    hidden, scaled = attend(where, mixed, tokens, out_all)

    scaled_flat = scaled.reshape(items * LENGTH, WIDTH)
    grad_flat = cotangent.reshape(items * LENGTH, WIDTH)
    before = ()
    ups, downs = [], []
    for k in range(slices):
        out, back, grad_up, grad_down = feed(scaled_flat, grad_flat, up_all[k], down_all[k], before)
        before = (out, back)
        ups.append(grad_up)
        downs.append(grad_down)
    result, grad_hidden, grads_out, grad_out_w, gain_two_sum = finish(
        where, before[0], before[1], hidden, cotangent, out_all, mixed
    )
    grads = exchange(grads_out)
    back_values, grad_logits = mix_back(
        lengths_here, offsets, grads, values, mixed_out, sums, logits_parts, shares
    )
    grad_mixer = lax.psum_scatter(grad_logits[0][0], "seq", scatter_dimension=1, tiled=True)
    grad_mixer = grad_mixer.astype(f32) * logits
    grad_values = exchange(back_values)
    grad_tokens, grad_value_w, gain_one_sum = grad_tokens_of(
        where, tokens, grad_hidden, value_all, grad_values
    )

    gains = jnp.concatenate(
        [gain_one_sum.reshape(ranks, 1, shard), gain_two_sum.reshape(ranks, 1, shard)], axis=2
    )
    gains = jnp.pad(gains, ((0, 0), (0, 7), (0, WIDTH - 2 * shard))).astype(bf16)
    payload = jnp.concatenate(
        [
            grad_out_w.reshape(ranks, shard, WIDTH),
            jnp.stack([u.reshape(ranks, shard, WIDTH) for u in ups], axis=2).reshape(
                ranks, shard * slices, WIDTH
            ),
            jnp.stack(downs).reshape(ranks, shard * slices, WIDTH),
            grad_value_w.reshape(ranks, shard, WIDTH),
            gains,
        ],
        axis=1,
    )
    payload = lax.psum_scatter(payload, ALL, scatter_dimension=0, tiled=False).astype(f32)
    at = shard
    sum_out = payload[:at]
    sum_up = payload[at : at + shard * slices].reshape(shard, HIDDEN) * second_gain
    at += shard * slices
    sum_down = payload[at : at + shard * slices]
    at += shard * slices
    sum_value = payload[at : at + shard] * first_gain
    at += shard
    sum_gain_one = payload[at, :shard] / first_gain[:, 0]
    sum_gain_two = payload[at, shard : 2 * shard] / second_gain[:, 0]
    return (
        result,
        grad_tokens,
        grad_mixer,
        sum_gain_one,
        sum_gain_two,
        sum_value,
        sum_out,
        sum_up,
        sum_down,
    )


def solution(mesh):
    rows = P(ALL, None)
    line = P(ALL)
    cube = P(ALL, None, None)
    logits = P("dp", "seq", None)
    return jax.shard_map(
        functools.partial(body, groups=mesh.shape["dp"], seqs=mesh.shape["seq"]),
        mesh=mesh,
        in_specs=(cube, line, logits, line, line, rows, rows, rows, rows, cube),
        out_specs=(cube, cube, logits, line, line, rows, rows, rows, rows),
        check_vma=False,
    )
```

```python
import functools

import jax
import jax.numpy as jnp
from jax import lax
from jax.experimental import pallas as pl
from jax.experimental.pallas import tpu as pltpu
from jax.sharding import PartitionSpec as P

epsilon = 1e-06
bf16 = jnp.bfloat16
f32 = jnp.float32
WIDTH = 768
LENGTH = 1024
HIDDEN = 3072
HEADS = 12
HEAD_DIM = 64
CHUNKS = 2


def rows_by_rows(left, right):
    return lax.dot_general(left, right, (((1,), (1,)), ((), ())), preferred_element_type=f32)


def times(left, right):
    return jnp.dot(left, right, preferred_element_type=f32)


def rms(values):
    return lax.rsqrt(jnp.mean(values * values, axis=-1, keepdims=True) + epsilon)


def share(offsets, at, refs, source):
    for ref in refs:
        count, rows, _ = ref.shape
        for k in range(count):
            ref[k] = source[pl.ds(pl.multiple_of(offsets[at], 16), rows), :]
            at += 1
    return at


def share_two(core, offsets, at, keeps, sends, first, second):
    @pl.when(core == 0)
    def _():
        share(offsets, at, keeps, first)
        share(offsets, at, sends, second)

    @pl.when(core != 0)
    def _():
        share(offsets, at, keeps, second)
        share(offsets, at, sends, first)


VMEM = 59 * 1024 * 1024
SCALE = 0.001
ANY = pl.BlockSpec(memory_space=pl.ANY)
ALL = ("dp", "seq")
FIRST = 0.7978845608028654
SECOND = FIRST * 0.044715


def call(kernel, name, grid, scalars, operands, outputs, scratch, flops, moved, after=(), aliases=None):
    count = len(scalars) + len(operands)

    def run(*refs):
        kernel(*refs[:count], *refs[count + len(after) :])

    return pl.pallas_call(
        run,
        grid_spec=pltpu.PrefetchScalarGridSpec(
            num_scalar_prefetch=len(scalars),
            grid=grid,
            in_specs=[block for _, block in operands] + [ANY] * len(after),
            out_specs=[block for _, block in outputs],
            scratch_shapes=scratch,
        ),
        out_shape=[shape for shape, _ in outputs],
        input_output_aliases=aliases or {},
        compiler_params=pltpu.CompilerParams(vmem_limit_bytes=VMEM),
        cost_estimate=pl.CostEstimate(
            flops=int(flops * SCALE), bytes_accessed=int(moved * SCALE), transcendentals=0
        ),
        name=name,
    )(*scalars, *[array for array, _ in operands], *after)


def shape(*sizes, kind=bf16):
    return jax.ShapeDtypeStruct(sizes, kind)


def spread(scratch, refs, place):
    for at, ref in enumerate(refs):
        group = ref.shape[0]
        scratch[pl.ds(pl.multiple_of((place ^ at) * group, 64), group), :] = ref[...]


def pick(scratch, refs, place):
    for at, ref in enumerate(refs):
        group = ref.shape[0]
        ref[...] = scratch[pl.ds(pl.multiple_of((place ^ at) * group, 64), group), :]


def values_kernel(where, offsets, x_ref, *rest, pieces, groups):
    parts, rest = rest[:pieces], rest[pieces:]
    outs, (w_ref, turned, scratch, sem) = rest[:groups], rest[groups:]
    step = pl.program_id(0)

    @pl.when(step == 0)
    def _():
        load_weight(offsets, parts, w_ref, sem)
        turned[...] = w_ref[...].T

    for half in range(2):
        at = pl.ds(half * LENGTH // 2, LENGTH // 2)
        x = x_ref[0, at, :].astype(f32)
        scaled = (x * rms(x)).astype(bf16)
        scratch[:, at] = rows_by_rows(turned[...], scaled).astype(bf16)
    pick(scratch, [out.at[0] for out in outs], where[0])


def project_values(where, offsets, tokens, parts, groups, after):
    items = tokens.shape[0]
    group = WIDTH // groups
    units = sum(p.shape[0] for p in parts)
    whole = lambda *_: (0, 0)
    outs = call(
        functools.partial(values_kernel, pieces=len(parts), groups=groups),
        "project_values",
        (items,),
        [where, offsets],
        [(tokens, pl.BlockSpec((1, LENGTH, WIDTH), lambda i, *_: (i, 0, 0)))]
        + [(p, ANY) for p in parts],
        [(shape(items, group, LENGTH), pl.BlockSpec((1, group, LENGTH), lambda i, *_: (i, 0, 0)))] * groups
        + [(shape(WIDTH, WIDTH), pl.BlockSpec((WIDTH, WIDTH), whole))],
        [
            pltpu.VMEM((WIDTH, WIDTH), bf16),
            pltpu.VMEM((WIDTH, LENGTH), bf16),
            pltpu.SemaphoreType.DMA((units,)),
        ],
        2 * items * LENGTH * WIDTH * WIDTH,
        4 * items * LENGTH * WIDTH,
        after,
    )
    return outs[:groups], outs[groups]


def load_logits(offsets, pieces, held, sems):
    def copy(head, at):
        rows = pieces[at].shape[1]
        start = pl.multiple_of(offsets[at], rows)
        return pltpu.make_async_copy(
            pieces[at].at[head], held.at[head, pl.ds(start, rows)], sems.at[head, at]
        )

    head = pl.program_id(0)

    @pl.when(head == 0)
    def _():
        for h in range(held.shape[0]):
            for at in range(len(pieces)):
                copy(h, at).start()

    for at in range(len(pieces)):
        copy(head, at).wait()


def reach(lengths, base, count):
    which = lax.broadcasted_iota(jnp.int32, (16, LENGTH), 0)
    ends = jnp.zeros((16, LENGTH), jnp.int32)
    for k in range(count):
        ends = jnp.where(which == k, lengths[base + k], ends)
    return jnp.where(lax.broadcasted_iota(jnp.int32, (16, LENGTH), 1) < ends, 1.0, 0.0)


def keep_of(lengths, k):
    return lax.broadcasted_iota(jnp.int32, (1, LENGTH), 1) < lengths[k]


def mix_kernel(lengths, offsets, *rest, groups, pieces, base):
    values, parts = rest[:groups], rest[groups : groups + pieces]
    outs = rest[groups + pieces : 2 * groups + pieces]
    sums_ref, held, left, sems = rest[2 * groups + pieces :]
    load_logits(offsets, parts, held, sems)
    for k in range(groups):
        block = values[k][0]
        left[pl.ds(k * HEAD_DIM, HEAD_DIM), :] = jnp.where(
            keep_of(lengths, base + k), block, jnp.zeros_like(block)
        )
    left[pl.ds(groups * HEAD_DIM, 16), :] = reach(lengths, base, groups).astype(bf16)
    product = rows_by_rows(left[...], held[pl.program_id(0)])
    sums = product[groups * HEAD_DIM : groups * HEAD_DIM + 8]
    sums_ref[0] = sums
    for k in range(groups):
        mixed = product[k * HEAD_DIM : (k + 1) * HEAD_DIM] / sums[k : k + 1]
        outs[k][...] = jnp.where(keep_of(lengths, base + k), mixed, 0.0).astype(bf16)


def mix_items(lengths, offsets, values, parts, item, after=()):
    groups, pieces = len(values), len(parts)
    group = values[0].shape[1]
    base = item * groups
    heads = group // HEAD_DIM
    block = pl.BlockSpec((HEAD_DIM, LENGTH), lambda h, *_: (h, 0))
    outs = call(
        functools.partial(mix_kernel, groups=groups, pieces=pieces, base=base),
        "mix_items",
        (heads,),
        [lengths, offsets],
        [(v, pl.BlockSpec((1, HEAD_DIM, LENGTH), lambda h, *_: (item, h, 0))) for v in values] + [(p, ANY) for p in parts],
        [(shape(group, LENGTH), block)] * groups
        + [(shape(heads, 8, LENGTH, kind=f32), pl.BlockSpec((1, 8, LENGTH), lambda h, *_: (h, 0, 0)))],
        [
            pltpu.VMEM((heads, LENGTH, LENGTH), bf16),
            pltpu.VMEM((groups * HEAD_DIM + 16, LENGTH), bf16),
            pltpu.SemaphoreType.DMA((heads, pieces)),
        ],
        2 * heads * (groups * HEAD_DIM + 16) * LENGTH * LENGTH,
        12 << 20,
        after,
    )
    return outs[:groups], outs[groups]


def values_back_kernel(lengths, offsets, *rest, groups, pieces, base):
    grads, mixed, rest = rest[:groups], rest[groups : 2 * groups], rest[2 * groups :]
    sums_ref, parts = rest[0], rest[1 : 1 + pieces]
    outs = rest[1 + pieces : 1 + pieces + groups]
    left_ref, held, sems = rest[1 + pieces + groups :]
    load_logits(offsets, parts, held, sems)
    which = lax.broadcasted_iota(jnp.int32, (16, LENGTH), 0)
    extra = jnp.zeros((16, LENGTH), f32)
    for k in range(groups):
        keep = keep_of(lengths, base + k)
        inverse = jnp.where(keep, 1.0 / sums_ref[0, k : k + 1], 0.0)
        grad = grads[k][...].astype(f32)
        delta = jnp.sum(grad * mixed[k][...].astype(f32), axis=0, keepdims=True)
        left_ref[0, pl.ds(k * HEAD_DIM, HEAD_DIM), :] = (grad * inverse).astype(bf16)
        extra = jnp.where(which == k, -(delta * inverse), extra)
    left_ref[0, pl.ds(groups * HEAD_DIM, 16), :] = extra.astype(bf16)
    product = times(left_ref[0, pl.ds(0, groups * HEAD_DIM), :], held[pl.program_id(0)])
    for k in range(groups):
        part = product[k * HEAD_DIM : (k + 1) * HEAD_DIM]
        outs[k][...] = jnp.where(keep_of(lengths, base + k), part, 0.0).astype(bf16)


def values_back(lengths, offsets, grads, mixed, sums, parts, base, after=()):
    groups, pieces = len(grads), len(parts)
    group = grads[0].shape[0]
    heads = group // HEAD_DIM
    tall = groups * HEAD_DIM + 16
    block = pl.BlockSpec((HEAD_DIM, LENGTH), lambda h, *_: (h, 0))
    outs = call(
        functools.partial(values_back_kernel, groups=groups, pieces=pieces, base=base),
        "values_back",
        (heads,),
        [lengths, offsets],
        [(g, block) for g in grads]
        + [(m, block) for m in mixed]
        + [(sums, pl.BlockSpec((1, 8, LENGTH), lambda h, *_: (h, 0, 0)))]
        + [(p, ANY) for p in parts],
        [(shape(group, LENGTH), block)] * groups
        + [(shape(heads, tall, LENGTH), pl.BlockSpec((1, tall, LENGTH), lambda h, *_: (h, 0, 0)))],
        [
            pltpu.VMEM((heads, LENGTH, LENGTH), bf16),
            pltpu.SemaphoreType.DMA((heads, pieces)),
        ],
        2 * heads * tall * LENGTH * LENGTH,
        14 << 20,
        after,
    )
    return outs[:groups], outs[groups]


def logits_back_kernel(lengths, offsets, *rest, count, groups, shares):
    lefts, values, rest = rest[:count], rest[count : count + groups], rest[count + groups :]
    refs, (left, right, whole) = rest[: len(shares)], rest[len(shares) :]
    tall = groups * HEAD_DIM + 16
    for item in range(count):
        left[pl.ds(item * tall, tall), :] = lefts[item][0]
        for k in range(groups):
            block = values[k][item]
            right[pl.ds(item * tall + k * HEAD_DIM, HEAD_DIM), :] = jnp.where(
                keep_of(lengths, item * groups + k), block, jnp.zeros_like(block)
            )
        right[pl.ds(item * tall + groups * HEAD_DIM, 16), :] = reach(
            lengths, item * groups, groups
        ).astype(bf16)
    whole[...] = times(left[...].T, right[...]).astype(bf16)
    at = 0
    for ref, (number, rows) in zip(refs, shares):
        for k in range(number):
            ref[k, 0] = whole[pl.ds(pl.multiple_of(offsets[at], rows), rows), :]
            at += 1


def logits_back(lengths, offsets, lefts, values, shares, after=()):
    count, groups = len(lefts), len(values)
    heads, tall, _ = lefts[0].shape
    block = pl.BlockSpec((count, HEAD_DIM, LENGTH), lambda h, *_: (0, h, 0))
    return call(
        functools.partial(logits_back_kernel, count=count, groups=groups, shares=shares),
        "logits_back",
        (heads,),
        [lengths, offsets],
        [(v, pl.BlockSpec((1, tall, LENGTH), lambda h, *_: (h, 0, 0))) for v in lefts]
        + [(v, block) for v in values],
        [
            (
                shape(number, heads, rows, LENGTH),
                pl.BlockSpec((number, 1, rows, LENGTH), lambda h, *_: (0, h, 0, 0)),
            )
            for number, rows in shares
        ],
        [
            pltpu.VMEM((count * tall, LENGTH), bf16),
            pltpu.VMEM((count * tall, LENGTH), bf16),
            pltpu.VMEM((LENGTH, LENGTH), bf16),
        ],
        2 * heads * count * tall * LENGTH * LENGTH,
        14 << 20,
        after,
    )


def load_weight(offsets, pieces, held, sem):
    copies = []
    at = 0
    for piece in pieces:
        count, rows, columns = piece.shape
        for k in range(count):
            start = pl.multiple_of(offsets[2 * at], 16)
            side = pl.multiple_of(offsets[2 * at + 1], 128)
            copies.append(
                pltpu.make_async_copy(
                    piece.at[k], held.at[pl.ds(start, rows), pl.ds(side, columns)], sem.at[at]
                )
            )
            at += 1
    for copy in copies:
        copy.start()
    for copy in copies:
        copy.wait()


def halves(total, gain, low, high):
    half = WIDTH // 2
    column = jnp.broadcast_to(gain, (128, WIDTH)).T
    leading = column.astype(bf16)
    low[:, pl.ds(0, half)] = total[:, :half].astype(bf16)
    high[:, pl.ds(0, half)] = total[:, half:].astype(bf16)
    low[:, pl.ds(half, 128)] = leading
    high[:, pl.ds(half, 128)] = (column - leading.astype(f32)).astype(bf16)


class Refs:
    def __init__(self, refs):
        self.refs, self.at = refs, 0

    def take(self, count=None):
        if count is None:
            self.at += 1
            return self.refs[self.at - 1]
        self.at += count
        return self.refs[self.at - count : self.at]


def feed_kernel(where, units_at, pieces_at, *refs, first, last, carried, settled, plain, slices, groups, parts, pieces):
    refs = Refs(refs)
    grad_ref, weights = refs.take(), refs.take(pieces)
    mixed = refs.take(groups) if first or last else None
    w_ref = refs.take() if last and not first else None
    if first:
        x_ref = refs.take()
    else:
        hidden_ref, scaled_ref, out_ref, back_ref = refs.take(4)
    if carried:
        carry = refs.take(2 + 2 * last)
    if last and carried:
        refs.take()
    if first:
        hidden_out, scaled_out, w_out = refs.take(3)
    if last:
        result_ref, grad_hidden_ref, grads = refs.take(), refs.take(), refs.take(groups)
    else:
        out_next, back_next = refs.take(2)
    if settled and plain:
        joint = refs.take(1 + last)
    elif settled:
        keeps, sends = refs.take(parts[0]), refs.take(parts[1])
        if last:
            w_keeps, w_sends = refs.take(parts[0]), refs.take(parts[1])
    else:
        handed = refs.take(2 + 2 * last)
    held, up_turned, down_turned, active, grad_pre, sum_up, sum_down, sems, loaded = refs.take(9)
    if first or last:
        turned = refs.take()
    if last:
        scratch, sum_w, sum_gain, low, high = refs.take(5)
    step = pl.program_id(0)
    final = step == pl.num_programs(0) - 1
    units = slices * WIDTH
    up_ref = held.at[:, pl.ds(0, units)]
    down_ref = held.at[:, pl.ds(units, units)]
    downs = [held.at[:, pl.ds(units + q * WIDTH, WIDTH)] for q in range(slices)]
    if first:
        w_ref = held.at[:, pl.ds(2 * units, WIDTH)]
    sums = [sum_up, sum_down] + ([sum_w, sum_gain] if last else [])

    def bring():
        return [pltpu.make_async_copy(carry[k], sums[k], sems.at[k]) for k in range(len(sums))]

    @pl.when(step == 0)
    def _():
        if carried:
            for copy in bring():
                copy.start()
        else:
            for total in sums:
                total[...] = jnp.zeros_like(total)
        load_weight(pieces_at, weights, held, loaded)
        if first:
            w_out[...] = w_ref[...]
        up_turned[...] = up_ref[...].T
        for q in range(slices):
            down_turned[:, pl.ds(q * WIDTH, WIDTH)] = downs[q][...].T

    if first or last:
        spread(turned, mixed, where[0])
    if first:
        hidden = x_ref[0].astype(f32) + times(turned[...].T, w_ref[...])
        hidden_out[...] = hidden
        scaled = (hidden * rms(hidden)).astype(bf16)
        scaled_out[...] = scaled
    else:
        scaled = scaled_ref[...]
    grad = grad_ref[0]
    slab = 256
    for k in range(units // slab):
        at = pl.ds(k * slab, slab)
        inner = pl.ds(k * slab % WIDTH, slab)
        pre = rows_by_rows(up_turned[at, :], scaled)
        grad_active = rows_by_rows(downs[k * slab // WIDTH][inner, :], grad)
        square = pre * pre
        half = 0.5 + 0.5 * jnp.tanh(pre * (FIRST + SECOND * square))
        act = pre * half
        active[at, :] = act.astype(bf16)
        slope = half + act * (1.0 - half) * (2.0 * FIRST + 6.0 * SECOND * square)
        grad_pre[at, :] = (grad_active * slope).astype(bf16)
    out = times(down_turned[...], active[...])
    back = times(up_ref[...], grad_pre[...])
    if not first:
        out, back = out + out_ref[...], back + back_ref[...]
    if carried:

        @pl.when(step == 0)
        def _():
            for copy in bring():
                copy.wait()

    for q in range(slices):
        at = pl.ds(q * WIDTH, WIDTH)
        sum_down[at, :] += times(active[at, :], grad)
        sum_up[at, :] += times(grad_pre[at, :], scaled)
    if last:
        hidden = hidden if first else hidden_ref[...]
        result_ref[0] = (hidden + out.T).astype(bf16)
        weighted = back.T
        scale = rms(hidden)
        both = weighted * hidden
        mean = jnp.mean(both, axis=-1, keepdims=True)
        attended = (grad.astype(f32) + scale * weighted - hidden * (scale**3 * mean)).astype(bf16)
        grad_hidden_ref[...] = attended
        scratch[...] = rows_by_rows(w_ref[...], attended).astype(bf16)
        pick(scratch, grads, where[0])
        sum_w[...] += times(turned[...], attended)
        sum_gain[...] += jnp.sum(both * scale, axis=0, keepdims=True)
    else:
        out_next[...] = out
        back_next[...] = back

    @pl.when(final)
    def _():
        if settled:
            for q in range(slices):
                at = pl.ds(q * WIDTH, WIDTH)
                up_ref[:, at] = sum_up[at, :].T.astype(bf16)
                down_ref[:, at] = sum_down[at, :].astype(bf16)
            if last:
                halves(sum_w[...], sum_gain[...], low, high)
            if plain:
                joint[0][...] = held[:, pl.ds(0, 2 * units)]
                if last:
                    joint[1][:, pl.ds(0, low.shape[1])] = low[...]
                    joint[1][:, pl.ds(low.shape[1], low.shape[1])] = high[...]
            else:
                share_two(where[2], units_at, 0, keeps, sends, up_ref, down_ref)
                if last:
                    share_two(where[2], units_at, 0, w_keeps, w_sends, low, high)
        else:
            copies = [
                pltpu.make_async_copy(sums[k], handed[k], sems.at[k]) for k in range(len(sums))
            ]
            for copy in copies:
                copy.start()
            for copy in copies:
                copy.wait()


def feed(where, units_at, item, chunk, grad, packed, w_out, tokens, mixed, state, carry, earlier, shapes, settled, after=()):
    rows = 256
    groups, parts, plain = len(mixed), [len(kind) for kind in shapes or ()], shapes is None
    group = mixed[0].shape[0]
    first, last = chunk == 0, chunk == CHUNKS - 1
    slices = HIDDEN // CHUNKS // WIDTH
    units = slices * WIDTH
    once = pl.Buffered(1)
    tall = pl.BlockSpec((1, rows, WIDTH), lambda j, *_: (item, j, 0))
    flat = pl.BlockSpec((rows, WIDTH), lambda j, *_: (j, 0))
    wide = pl.BlockSpec((WIDTH, rows), lambda j, *_: (0, j))
    split = pl.BlockSpec((group, rows), lambda j, *_: (0, j))
    square = pl.BlockSpec((WIDTH, WIDTH), lambda j, *_: (0, 0), pipeline_mode=once)
    weights, weights_at = packed
    operands = [(grad, tall)] + [(w, ANY) for w in weights]
    if first or last:
        operands += [(m, split) for m in mixed]
    if last and not first:
        operands += [(w_out, square)]
    if first:
        operands += [(tokens, tall)]
    else:
        operands += list(zip(state, (flat, flat, wide, wide)))
    aliases = {}
    if carry:
        operands += [(c, ANY) for c in carry]
    outputs = []
    if first:
        outputs += [(shape(LENGTH, WIDTH, kind=f32), flat), (shape(LENGTH, WIDTH), flat), (shape(WIDTH, WIDTH), square)]
    if last:
        if carry:
            aliases = {3 + len(operands): len(outputs)}
            operands += [(e, ANY) for e in earlier]
        outputs += [(shape(*grad.shape), tall), (shape(LENGTH, WIDTH), flat)]
        outputs += [(shape(group, LENGTH), split)] * groups
    else:
        outputs += [(shape(WIDTH, LENGTH, kind=f32), wide)] * 2
    fixed = len(outputs)
    if settled:
        if plain:
            sizes = [shape(WIDTH, 2 * units), shape(WIDTH, WIDTH + 256)][: 1 + last]
        else:
            sizes = [shape(c, r, units) for kind in shapes for c, r in kind]
            if last:
                sizes += [shape(c, r, WIDTH // 2 + 128) for kind in shapes for c, r in kind]
        outputs += [
            (u, pl.BlockSpec(u.shape, lambda j, *_, n=len(u.shape): (0,) * n, pipeline_mode=once))
            for u in sizes
        ]
    else:
        sizes = [shape(units, WIDTH, kind=f32)] * 2
        if last:
            sizes += [shape(WIDTH, WIDTH, kind=f32), shape(1, WIDTH, kind=f32)]
        outputs += [(u, ANY) for u in sizes]
    scratch = [
        pltpu.VMEM((WIDTH, 2 * units + WIDTH * first), bf16),
        pltpu.VMEM((units, WIDTH), bf16),
        pltpu.VMEM((WIDTH, units), bf16),
        pltpu.VMEM((units, rows), bf16),
        pltpu.VMEM((units, rows), bf16),
        pltpu.VMEM((units, WIDTH), f32),
        pltpu.VMEM((units, WIDTH), f32),
        pltpu.SemaphoreType.DMA((4,)),
        pltpu.SemaphoreType.DMA((sum(w.shape[0] for w in weights),)),
    ]
    if first or last:
        scratch += [pltpu.VMEM((WIDTH, rows), bf16)]
    if last:
        scratch += [
            pltpu.VMEM((WIDTH, rows), bf16),
            pltpu.VMEM((WIDTH, WIDTH), f32),
            pltpu.VMEM((1, WIDTH), f32),
            pltpu.VMEM((WIDTH, WIDTH // 2 + 128), bf16),
            pltpu.VMEM((WIDTH, WIDTH // 2 + 128), bf16),
        ]
    outs = call(
        functools.partial(
            feed_kernel,
            first=first,
            last=last,
            carried=bool(carry),
            settled=settled,
            plain=plain,
            slices=slices,
            groups=groups,
            parts=parts,
            pieces=len(weights),
        ),
        "feed",
        (LENGTH // rows,),
        [where, units_at, weights_at],
        operands,
        outputs,
        scratch,
        12 * LENGTH * WIDTH * units,
        20 << 20,
        after,
        aliases,
    )
    main, sums = outs[:fixed], outs[fixed:]
    if settled and not plain:
        keep, both = parts[0], sum(parts)
        sums = [(sums[at : at + keep], sums[at + keep : at + both]) for at in range(0, len(sums), both)]
    return main, sums


def tokens_kernel(where, units_at, *refs, groups, parts, carried, settled, plain):
    refs = Refs(refs)
    x_ref, grad_ref, w_ref, grads = refs.take(), refs.take(), refs.take(), refs.take(groups)
    if carried:
        carry = refs.take(2)
        refs.take()
    result_ref = refs.take()
    if settled and plain:
        joint = refs.take()
    elif settled:
        keeps, sends = refs.take(parts[0]), refs.take(parts[1])
    else:
        handed = refs.take(2)
    turned, sum_w, sum_gain, low, high, sems = refs.take(6)
    step = pl.program_id(0)
    sums = [sum_w, sum_gain]

    @pl.when(step == 0)
    def _():
        if carried:
            copies = [pltpu.make_async_copy(carry[k], sums[k], sems.at[k]) for k in range(2)]
            for copy in copies:
                copy.start()
            for copy in copies:
                copy.wait()
        else:
            for total in sums:
                total[...] = jnp.zeros_like(total)

    spread(turned, grads, where[0])
    x = x_ref[0].astype(f32)
    scale = rms(x)
    scaled = (x * scale).astype(bf16)
    weighted = rows_by_rows(turned[...].T, w_ref[...])
    both = weighted * x
    mean = jnp.mean(both, axis=-1, keepdims=True)
    total = grad_ref[...].astype(f32) + scale * weighted - x * (scale**3 * mean)
    result_ref[0] = total.astype(bf16)
    sum_gain[...] += jnp.sum(both * scale, axis=0, keepdims=True)
    sum_w[...] += times(turned[...], scaled)

    @pl.when(step == pl.num_programs(0) - 1)
    def _():
        if settled:
            halves(sum_w[...].T, sum_gain[...], low, high)
            if plain:
                joint[:, pl.ds(0, low.shape[1])] = low[...]
                joint[:, pl.ds(low.shape[1], low.shape[1])] = high[...]
            else:
                share_two(where[2], units_at, 0, keeps, sends, low, high)
        else:
            copies = [pltpu.make_async_copy(sums[k], handed[k], sems.at[k]) for k in range(2)]
            for copy in copies:
                copy.start()
            for copy in copies:
                copy.wait()


def grad_tokens_of(where, units_at, item, tokens, grad_hidden, weight, grads, carry, earlier, shapes, settled, after=()):
    rows = 256
    groups, parts, plain = len(grads), [len(kind) for kind in shapes or ()], shapes is None
    group = grads[0].shape[0]
    tall = pl.BlockSpec((1, rows, WIDTH), lambda j, *_: (item, j, 0))
    whole = lambda j, *_: (0, 0)
    operands = [
        (tokens, tall),
        (grad_hidden, pl.BlockSpec((rows, WIDTH), lambda j, *_: (j, 0))),
        (weight, pl.BlockSpec((WIDTH, WIDTH), whole)),
    ] + [(g, pl.BlockSpec((group, rows), lambda j, *_: (0, j))) for g in grads]
    aliases = {}
    if carry:
        operands += [(c, ANY) for c in carry]
        aliases = {2 + len(operands): 0}
        operands += [(earlier, ANY)]
    outputs = [(shape(*tokens.shape), tall)]
    half = WIDTH // 2 + 128
    if settled:
        sizes = [shape(c, r, half) for kind in shapes or () for c, r in kind]
        outputs += [(u, pl.BlockSpec(u.shape, lambda j, *_: (0, 0, 0))) for u in sizes]
        if plain:
            outputs += [(shape(WIDTH, 2 * half), pl.BlockSpec((WIDTH, 2 * half), whole))]
    else:
        outputs += [(shape(WIDTH, WIDTH, kind=f32), ANY), (shape(1, WIDTH, kind=f32), ANY)]
    outs = call(
        functools.partial(tokens_kernel, groups=groups, parts=parts, carried=bool(carry), settled=settled, plain=plain),
        "grad_tokens",
        (LENGTH // rows,),
        [where, units_at],
        operands,
        outputs,
        [
            pltpu.VMEM((WIDTH, rows), bf16),
            pltpu.VMEM((WIDTH, WIDTH), f32),
            pltpu.VMEM((1, WIDTH), f32),
            pltpu.VMEM((WIDTH, half), bf16),
            pltpu.VMEM((WIDTH, half), bf16),
            pltpu.SemaphoreType.DMA((2,)),
        ],
        4 * LENGTH * WIDTH * WIDTH,
        8 << 20,
        after,
        aliases,
    )
    if settled and not plain:
        return outs[0], (outs[1 : 1 + parts[0]], outs[1 + parts[0] :])
    return outs[0], outs[1:]


def halved(array):
    half = array.shape[1] // 2
    return array[:, :half], array[:, half:]


def hold(*values):
    return lax.optimization_barrier(values)


def exchange(parts):
    got = [parts[0]]
    for r in range(1, len(parts)):
        got.append(lax.ppermute(parts[r], "dp", [(i, i ^ r) for i in range(len(parts))]))
    return got


def add(*terms):
    return functools.reduce(jnp.add, [t.astype(f32) for t in terms]).astype(bf16)


class Chips:
    def __init__(self, groups, seqs):
        self.groups, self.seqs, self.rings = groups, seqs, seqs // 2
        self.here, self.row = lax.axis_index("dp"), lax.axis_index("seq")
        self.core, self.z = self.row % 2, self.row // 2

    def across(self, array):
        return lax.ppermute(array, "seq", [(i, i ^ 1) for i in range(self.seqs)])

    def along(self, array, step):
        n = self.seqs
        return lax.ppermute(array, "seq", [(i, (i + 2 * step) % n) for i in range(n)])

    def over(self, array, bits):
        return lax.ppermute(array, "dp", [(i, i ^ bits) for i in range(self.groups)])

    def hop(self, array, step):
        return lax.ppermute(array, "seq", [(i, i ^ (2 * step)) for i in range(self.seqs)])

    def chip(self, bits, step):
        return (self.here ^ bits) * self.rings + (self.z ^ step)

    def chips(self):
        return [self.chip(b, s) for b in range(self.groups) for s in range(self.rings)]

    def gather_line(self, mine):
        return jnp.stack([mine] + [self.hop(mine, s) for s in range(1, self.rings)])

    def gather_plane(self, ring):
        return [ring] + [self.over(ring, bits) for bits in range(1, self.groups)]

    def gathered_at(self, rows):
        return jnp.stack([v for c in self.chips() for v in (c * rows, 0 * c)]).astype(jnp.int32)

    def unit_order(self, rows):
        return jnp.stack([c * rows for c in self.chips()]).astype(jnp.int32)

    def scatter_core(self, shares):
        keeps, (send,) = shares
        got, n = self.across(send), self.rings
        return [add(keep, got[b * n : (b + 1) * n]) for b, keep in enumerate(keeps)]

    def scatter_plane(self, parts):
        parts = [parts[0]] + [self.over(parts[b], b) for b in range(1, self.groups)]
        return [add(*[part[s] for part in parts]) for s in range(self.rings)]

    def scatter_line(self, own):
        return add(own[0], *[self.hop(own[s], s) for s in range(1, self.rings)])

    def settle(self, total):
        rows = total.shape[0] // 2
        mine = lax.dynamic_slice_in_dim(total, self.core * rows, rows)
        other = self.across(lax.dynamic_slice_in_dim(total, (1 - self.core) * rows, rows))
        first = self.core == 0
        return jnp.where(first, mine, other), jnp.where(first, other, mine)


def body(tokens, lengths, mixer, gain_one, gain_two, w_value, w_out, w_up, w_down, cotangent, groups, seqs):
    ranks = groups * seqs
    fast = groups == 4 and seqs == 8
    chips = Chips(groups, seqs)
    here, row, core = chips.here, chips.row, chips.core
    where = jnp.stack([here, row, core]).astype(jnp.int32)
    items = tokens.shape[0]
    shard = w_value.shape[0]
    slices = HIDDEN // WIDTH
    width = slices // CHUNKS
    half = WIDTH // 2

    first_gain = gain_one.astype(f32)[:, None]
    second_gain = gain_two.astype(f32)[:, None]
    value_mine = (w_value.astype(f32) * first_gain).astype(bf16)
    up_mine = (w_up.astype(f32) * second_gain).astype(bf16)
    up_mine = up_mine.reshape(shard, ranks, slices, shard).swapaxes(1, 2)
    down_mine = w_down.reshape(slices, shard, WIDTH).swapaxes(0, 1)
    weights = [value_mine]
    for chunk in range(CHUNKS):
        at = slice(chunk * width, (chunk + 1) * width)
        columns = [m[:, at].reshape(shard, width * WIDTH) for m in (up_mine, down_mine)]
        weights.append(jnp.concatenate(columns + [w_out][chunk:], axis=1))

    logits = jnp.exp(mixer.astype(f32))
    logits_low = logits.astype(bf16)
    block = logits.shape[1]
    shares_at, shares = [0], ((1, LENGTH),)
    whole = [lax.all_gather(w, ALL, axis=0, tiled=True)[None] for w in weights[fast:]]
    weights_at = [jnp.zeros((2,), jnp.int32)] * (1 + CHUNKS)
    if fast:
        rings = chips.rings
        whole = [None] + whole
        value_mine, lengths_here = hold(value_mine, exchange([lengths] * groups))
        other = chips.across(value_mine)
        value_unit = jnp.where(
            core == 0, jnp.concatenate([value_mine, other]), jnp.concatenate([other, value_mine])
        )
        weights_at[0] = chips.gathered_at(2 * shard)
        zs = [(chips.z - s) % rings for s in range(rings)]
        logits_at = [(2 * z + c) * block for c in (core, 1 - core) for z in zs]
        shapes = (((rings, 2 * shard),) * groups, ((groups * rings, 2 * shard),))
        order = chips.unit_order(2 * shard)
    else:
        value_parts = whole[:1]
        logits_parts = [lax.all_gather(logits_low, "seq", axis=1, tiled=True)]
        logits_at = [0]
        shapes = None
        order = jnp.zeros((1,), jnp.int32)
    logits_at, shares_at = (
        jnp.stack([jnp.asarray(v, jnp.int32) for v in at]) for at in (logits_at, shares_at)
    )
    if not fast:
        lengths_here = exchange([lengths] * groups)
    lengths_here = jnp.stack(lengths_here, axis=1).reshape(-1)

    def values_of(after=()):
        return project_values(where, weights_at[0], tokens, value_parts, groups, after)

    def mix(item, values, after=()):
        return mix_items(lengths_here, logits_at, values, logits_parts, item, after)

    def run_feed(item, chunk, packed, w_out_all, mixed, state, carry, result, after=()):
        return feed(
            where, order, item, chunk, cotangent, (packed, weights_at[1 + chunk]), w_out_all, tokens,
            mixed, state, carry, (result,), shapes if chunk else None, item == items - 1, after,
        )

    def back(item, grads, mixed_out, sums, after=()):
        return values_back(
            lengths_here, logits_at, grads, mixed_out, sums, logits_parts, item * groups, after
        )

    def close(item, grad_hidden, grads, carry, earlier, after=()):
        return grad_tokens_of(
            where, order, item, tokens, grad_hidden, value_all, grads, carry, earlier, shapes,
            item == items - 1, after,
        )

    if fast:
        assert items == 2 and CHUNKS == 2
        value_ring = chips.gather_line(value_unit)
        value_ring, logits_low = hold(value_ring, logits_low)
        value_parts = chips.gather_plane(value_ring)
        ring_one = chips.along(logits_low, 1)
        values, value_all = values_of()
        values, ring_one = hold(values, ring_one)
        values = exchange(values)
        ring_two = chips.along(ring_one, 1)
        cross_zero = chips.across(logits_low)
        values, ring_two, cross_zero = hold(values, ring_two, cross_zero)
        ring_three = chips.along(ring_two, 1)
        cross_one, cross_two = chips.across(ring_one), chips.across(ring_two)
        ring_three, cross_one, cross_two = hold(ring_three, cross_one, cross_two)
        logits_parts = [logits_low, ring_one, ring_two, ring_three]
        logits_parts += [cross_zero, cross_one, cross_two, chips.across(ring_three)]
        mixed_out_a, sums_a = mix(0, values)
        mixed_out_a, sums_a = hold(mixed_out_a, sums_a)
        mixed_a = exchange(mixed_out_a)
        mixed_out_b, sums_b = mix(1, values)
        mixed_out_b, mixed_a = hold(mixed_out_b, mixed_a)
        mixed_b = exchange(mixed_out_b)
        state_a, carry = run_feed(0, 0, whole[1:2], None, mixed_a, None, (), None)
        state_a, carry, mixed_b = hold(state_a, carry, mixed_b)
        w_out_all = state_a[2]
        state_b, (shared,) = run_feed(1, 0, whole[1:2], None, mixed_b, None, carry, None)
        first_sums = lax.psum_scatter(shared, ALL, scatter_dimension=0, tiled=True)
        state_a = state_a[:2] + state_a[3:]
        state_b = state_b[:2] + state_b[3:]
        out_a, carry = run_feed(0, 1, whole[2:3], w_out_all, mixed_a, state_a, (), None)
        out_a, carry = hold(out_a, carry)
        grads_a = exchange(out_a[2:])
        out_b, (second_shared, out_shared) = run_feed(
            1, 1, whole[2:3], w_out_all, mixed_b, state_b, carry, out_a[0]
        )
        out_b, grads_a, second_shared, out_shared = hold(out_b, grads_a, second_shared, out_shared)
        result = out_b[0]
        grads_b = exchange(out_b[2:])
        back_a, left_a = back(0, grads_a, mixed_out_a, sums_a)
        back_a, left_a, grads_b, second_shared, out_shared = hold(
            back_a, left_a, grads_b, second_shared, out_shared
        )
        back_a = exchange(back_a)
        back_b, left_b = back(1, grads_b, mixed_out_b, sums_b)
        second_sums = chips.scatter_core(second_shared)
        back_b, left_b, second_sums = hold(back_b, left_b, second_sums)
        back_b = exchange(back_b)
        grad_logits = logits_back(lengths_here, shares_at, [left_a, left_b], values, shares)
        grad_logits, back_a, second_sums, out_shared = hold(grad_logits, back_a, second_sums, out_shared)
        grad_mixer = lax.psum_scatter(grad_logits[0][0], "seq", scatter_dimension=1, tiled=True)
        grad_tokens, carry = close(0, out_a[1], back_a, (), None)
        carry, back_b, grad_tokens, second_sums, out_shared = hold(
            carry, back_b, grad_tokens, second_sums, out_shared
        )
        second_sums = chips.scatter_plane(second_sums)
        out_sums = chips.scatter_core(out_shared)
        grad_tokens, shared = close(1, out_b[1], back_b, carry, grad_tokens)
        shared, second_sums, out_sums = hold(shared, second_sums, out_sums)
        second_sums = chips.scatter_line(second_sums)
        value_sums = chips.scatter_core(shared)
        small_sums = [jnp.concatenate(pair, axis=2) for pair in zip(value_sums, out_sums)]
        small_sums, second_sums = hold(small_sums, second_sums)
        small_sums = chips.scatter_plane(small_sums)
        second_sums = chips.settle(second_sums)
        small_sums, second_sums = hold(small_sums, second_sums)
        low, high = chips.settle(chips.scatter_line(small_sums))
        small = half + 128
        settled = [halved(first_sums), second_sums, (low[:, small:], high[:, small:]), (low[:, :small], high[:, :small])]
    else:
        values, value_all = values_of()
        values = exchange(values)
        mixed_out, sums, mixed = [], [], []
        for item in range(items):
            out, total = mix(item, values)
            mixed_out.append(out)
            sums.append(total)
            mixed.append(exchange(out))
        states, w_out_all, result = [None] * items, None, None
        grads, grad_hidden, shared = [None] * items, [None] * items, []
        for chunk in range(CHUNKS):
            carry = ()
            for item in range(items):
                state, carry = run_feed(
                    item, chunk, whole[1 + chunk : 2 + chunk], w_out_all, mixed[item], states[item], carry, result
                )
                if chunk == CHUNKS - 1:
                    result, grad_hidden[item], grads[item] = state[0], state[1], exchange(state[2:])
                elif chunk == 0:
                    if item == items - 1:
                        w_out_all = state[2]
                    states[item] = list(state[:2]) + list(state[3:])
                else:
                    states[item] = list(states[item][:2]) + list(state)
            shared += carry
        lefts, grad_values = [], []
        for item in range(items):
            out, left = back(item, grads[item], mixed_out[item], sums[item])
            lefts.append(left)
            grad_values.append(exchange(out))
        grad_logits = logits_back(lengths_here, shares_at, lefts, values, shares)
        carry, grad_tokens = (), None
        for item in range(items):
            grad_tokens, carry = close(item, grad_hidden[item], grad_values[item], carry, grad_tokens)
        shared += carry
        grad_mixer = lax.psum_scatter(grad_logits[0][0], "seq", scatter_dimension=1, tiled=True)
        settled = [halved(lax.psum_scatter(x, ALL, scatter_dimension=0, tiled=True)) for x in shared]
    grad_mixer = grad_mixer.astype(f32) * logits
    ups = jnp.concatenate([pair[0] for pair in settled[:CHUNKS]], axis=1)
    downs = jnp.concatenate([pair[1] for pair in settled[:CHUNKS]], axis=1)
    sum_up = ups.astype(f32).reshape(shard, slices, ranks, shard).swapaxes(1, 2).reshape(shard, HIDDEN)
    sum_up = sum_up * second_gain
    sum_down = downs.astype(f32).reshape(shard, slices, WIDTH).swapaxes(0, 1).reshape(shard * slices, WIDTH)

    def joined(pair):
        low, high = (part.astype(f32) for part in pair)
        return jnp.concatenate([low[:, :half], high[:, :half]], axis=1), low[:, half] + high[:, half]

    sum_out, gain_two_sum = joined(settled[CHUNKS])
    sum_value, gain_one_sum = joined(settled[CHUNKS + 1])
    return (
        result,
        grad_tokens,
        grad_mixer,
        gain_one_sum / first_gain[:, 0],
        gain_two_sum / second_gain[:, 0],
        sum_value * first_gain,
        sum_out,
        sum_up,
        sum_down,
    )


def solution(mesh):
    rows = P(ALL, None)
    line = P(ALL)
    cube = P(ALL, None, None)
    logits = P("dp", "seq", None)
    return jax.shard_map(
        functools.partial(body, groups=mesh.shape["dp"], seqs=mesh.shape["seq"]),
        mesh=mesh,
        in_specs=(cube, line, logits, line, line, rows, rows, rows, rows, cube),
        out_specs=(cube, cube, logits, line, line, rows, rows, rows, rows),
        check_vma=False,
    )
```

```python
import functools

import jax
import jax.numpy as jnp
from jax import lax
from jax.experimental import pallas as pl
from jax.experimental.pallas import tpu as pltpu
from jax.sharding import PartitionSpec as P

epsilon = 1e-06
bf16 = jnp.bfloat16
f32 = jnp.float32
WIDTH = 768
LENGTH = 1024
HIDDEN = 3072
HEADS = 12
HEAD_DIM = 64
CHUNKS = 2


def rows_by_rows(left, right):
    return lax.dot_general(left, right, (((1,), (1,)), ((), ())), preferred_element_type=f32)


def turned_by_rows(left, right):
    return lax.dot_general(left, right, (((0,), (1,)), ((), ())), preferred_element_type=f32)


def turned_times(left, right):
    return lax.dot_general(left, right, (((0,), (0,)), ((), ())), preferred_element_type=f32)


def times(left, right):
    return jnp.dot(left, right, preferred_element_type=f32)


def rms(values):
    return lax.rsqrt(jnp.mean(values * values, axis=-1, keepdims=True) + epsilon)


def share(offsets, at, refs, source):
    for ref in refs:
        count, rows, _ = ref.shape
        for k in range(count):
            ref[k] = source[pl.ds(pl.multiple_of(offsets[at], 16), rows), :]
            at += 1
    return at


def share_two(core, offsets, at, keeps, sends, first, second):
    @pl.when(core == 0)
    def _():
        share(offsets, at, keeps, first)
        share(offsets, at, sends, second)

    @pl.when(core != 0)
    def _():
        share(offsets, at, keeps, second)
        share(offsets, at, sends, first)


VMEM = 59 * 1024 * 1024
SCALE = 0.001
ANY = pl.BlockSpec(memory_space=pl.ANY)
ALL = ("dp", "seq")
FIRST = 0.7978845608028654
SECOND = FIRST * 0.044715


def call(kernel, name, grid, scalars, operands, outputs, scratch, flops, moved, after=(), aliases=None):
    count = len(scalars) + len(operands)

    def run(*refs):
        kernel(*refs[:count], *refs[count + len(after) :])

    return pl.pallas_call(
        run,
        grid_spec=pltpu.PrefetchScalarGridSpec(
            num_scalar_prefetch=len(scalars),
            grid=grid,
            in_specs=[block for _, block in operands] + [ANY] * len(after),
            out_specs=[block for _, block in outputs],
            scratch_shapes=scratch,
        ),
        out_shape=[shape for shape, _ in outputs],
        input_output_aliases=aliases or {},
        compiler_params=pltpu.CompilerParams(vmem_limit_bytes=VMEM),
        cost_estimate=pl.CostEstimate(
            flops=int(flops * SCALE), bytes_accessed=int(moved * SCALE), transcendentals=0
        ),
        name=name,
    )(*scalars, *[array for array, _ in operands], *after)


def shape(*sizes, kind=bf16):
    return jax.ShapeDtypeStruct(sizes, kind)


def spread(scratch, refs, place):
    for at, ref in enumerate(refs):
        group = ref.shape[0]
        scratch[pl.ds(pl.multiple_of((place ^ at) * group, 64), group), :] = ref[...]


def pick(scratch, refs, place):
    for at, ref in enumerate(refs):
        group = ref.shape[0]
        ref[...] = scratch[pl.ds(pl.multiple_of((place ^ at) * group, 64), group), :]


def values_kernel(where, offsets, x_ref, *rest, pieces, groups):
    parts, rest = rest[:pieces], rest[pieces:]
    outs, (w_ref, turned, scratch, sem) = rest[:groups], rest[groups:]
    step = pl.program_id(0)

    @pl.when(step == 0)
    def _():
        load_weight(offsets, parts, w_ref, sem)
        turned[...] = w_ref[...].T

    for half in range(2):
        at = pl.ds(half * LENGTH // 2, LENGTH // 2)
        x = x_ref[0, at, :].astype(f32)
        scaled = (x * rms(x)).astype(bf16)
        scratch[:, at] = rows_by_rows(turned[...], scaled).astype(bf16)
    pick(scratch, [out.at[0] for out in outs], where[0])


def project_values(where, offsets, tokens, parts, groups, after):
    items = tokens.shape[0]
    group = WIDTH // groups
    units = sum(p.shape[0] for p in parts)
    whole = lambda *_: (0, 0)
    outs = call(
        functools.partial(values_kernel, pieces=len(parts), groups=groups),
        "project_values",
        (items,),
        [where, offsets],
        [(tokens, pl.BlockSpec((1, LENGTH, WIDTH), lambda i, *_: (i, 0, 0)))]
        + [(p, ANY) for p in parts],
        [(shape(items, group, LENGTH), pl.BlockSpec((1, group, LENGTH), lambda i, *_: (i, 0, 0)))] * groups
        + [(shape(WIDTH, WIDTH), pl.BlockSpec((WIDTH, WIDTH), whole))],
        [
            pltpu.VMEM((WIDTH, WIDTH), bf16),
            pltpu.VMEM((WIDTH, LENGTH), bf16),
            pltpu.SemaphoreType.DMA((units,)),
        ],
        2 * items * LENGTH * WIDTH * WIDTH,
        4 * items * LENGTH * WIDTH,
        after,
    )
    return outs[:groups], outs[groups]


def load_logits(offsets, pieces, held, sems):
    def copy(head, at):
        rows = pieces[at].shape[1]
        start = pl.multiple_of(offsets[at], rows)
        return pltpu.make_async_copy(
            pieces[at].at[head], held.at[head, pl.ds(start, rows)], sems.at[head, at]
        )

    head = pl.program_id(0)

    @pl.when(head == 0)
    def _():
        for h in range(held.shape[0]):
            for at in range(len(pieces)):
                copy(h, at).start()

    for at in range(len(pieces)):
        copy(head, at).wait()


def reach(lengths, base, count):
    which = lax.broadcasted_iota(jnp.int32, (16, LENGTH), 0)
    ends = jnp.zeros((16, LENGTH), jnp.int32)
    for k in range(count):
        ends = jnp.where(which == k, lengths[base + k], ends)
    return jnp.where(lax.broadcasted_iota(jnp.int32, (16, LENGTH), 1) < ends, 1.0, 0.0)


def keep_of(lengths, k):
    return lax.broadcasted_iota(jnp.int32, (1, LENGTH), 1) < lengths[k]


def mix_kernel(lengths, offsets, *rest, groups, pieces, base):
    values, parts = rest[:groups], rest[groups : groups + pieces]
    outs = rest[groups + pieces : 2 * groups + pieces]
    sums_ref, held, left, sems = rest[2 * groups + pieces :]
    load_logits(offsets, parts, held, sems)
    for k in range(groups):
        block = values[k][0]
        left[pl.ds(k * HEAD_DIM, HEAD_DIM), :] = jnp.where(
            keep_of(lengths, base + k), block, jnp.zeros_like(block)
        )
    left[pl.ds(groups * HEAD_DIM, 16), :] = reach(lengths, base, groups).astype(bf16)
    product = rows_by_rows(left[...], held[pl.program_id(0)])
    sums = product[groups * HEAD_DIM : groups * HEAD_DIM + 8]
    sums_ref[0] = sums
    for k in range(groups):
        mixed = product[k * HEAD_DIM : (k + 1) * HEAD_DIM] / sums[k : k + 1]
        outs[k][...] = jnp.where(keep_of(lengths, base + k), mixed, 0.0).astype(bf16)


def mix_items(lengths, offsets, values, parts, item, after=()):
    groups, pieces = len(values), len(parts)
    group = values[0].shape[1]
    base = item * groups
    heads = group // HEAD_DIM
    block = pl.BlockSpec((HEAD_DIM, LENGTH), lambda h, *_: (h, 0))
    outs = call(
        functools.partial(mix_kernel, groups=groups, pieces=pieces, base=base),
        "mix_items",
        (heads,),
        [lengths, offsets],
        [(v, pl.BlockSpec((1, HEAD_DIM, LENGTH), lambda h, *_: (item, h, 0))) for v in values] + [(p, ANY) for p in parts],
        [(shape(group, LENGTH), block)] * groups
        + [(shape(heads, 8, LENGTH, kind=f32), pl.BlockSpec((1, 8, LENGTH), lambda h, *_: (h, 0, 0)))],
        [
            pltpu.VMEM((heads, LENGTH, LENGTH), bf16),
            pltpu.VMEM((groups * HEAD_DIM + 16, LENGTH), bf16),
            pltpu.SemaphoreType.DMA((heads, pieces)),
        ],
        2 * heads * (groups * HEAD_DIM + 16) * LENGTH * LENGTH,
        12 << 20,
        after,
    )
    return outs[:groups], outs[groups]


def values_back_kernel(lengths, offsets, *rest, groups, pieces, base):
    grads, mixed, rest = rest[:groups], rest[groups : 2 * groups], rest[2 * groups :]
    sums_ref, parts = rest[0], rest[1 : 1 + pieces]
    outs = rest[1 + pieces : 1 + pieces + groups]
    left_ref, held, sems = rest[1 + pieces + groups :]
    load_logits(offsets, parts, held, sems)
    which = lax.broadcasted_iota(jnp.int32, (16, LENGTH), 0)
    extra = jnp.zeros((16, LENGTH), f32)
    for k in range(groups):
        keep = keep_of(lengths, base + k)
        inverse = jnp.where(keep, 1.0 / sums_ref[0, k : k + 1], 0.0)
        grad = grads[k][...].astype(f32)
        delta = jnp.sum(grad * mixed[k][...].astype(f32), axis=0, keepdims=True)
        left_ref[0, pl.ds(k * HEAD_DIM, HEAD_DIM), :] = (grad * inverse).astype(bf16)
        extra = jnp.where(which == k, -(delta * inverse), extra)
    left_ref[0, pl.ds(groups * HEAD_DIM, 16), :] = extra.astype(bf16)
    product = times(left_ref[0, pl.ds(0, groups * HEAD_DIM), :], held[pl.program_id(0)])
    for k in range(groups):
        part = product[k * HEAD_DIM : (k + 1) * HEAD_DIM]
        outs[k][...] = jnp.where(keep_of(lengths, base + k), part, 0.0).astype(bf16)


def values_back(lengths, offsets, grads, mixed, sums, parts, base, after=()):
    groups, pieces = len(grads), len(parts)
    group = grads[0].shape[0]
    heads = group // HEAD_DIM
    tall = groups * HEAD_DIM + 16
    block = pl.BlockSpec((HEAD_DIM, LENGTH), lambda h, *_: (h, 0))
    outs = call(
        functools.partial(values_back_kernel, groups=groups, pieces=pieces, base=base),
        "values_back",
        (heads,),
        [lengths, offsets],
        [(g, block) for g in grads]
        + [(m, block) for m in mixed]
        + [(sums, pl.BlockSpec((1, 8, LENGTH), lambda h, *_: (h, 0, 0)))]
        + [(p, ANY) for p in parts],
        [(shape(group, LENGTH), block)] * groups
        + [(shape(heads, tall, LENGTH), pl.BlockSpec((1, tall, LENGTH), lambda h, *_: (h, 0, 0)))],
        [
            pltpu.VMEM((heads, LENGTH, LENGTH), bf16),
            pltpu.SemaphoreType.DMA((heads, pieces)),
        ],
        2 * heads * tall * LENGTH * LENGTH,
        14 << 20,
        after,
    )
    return outs[:groups], outs[groups]


def logits_back_kernel(lengths, offsets, *rest, count, groups, shares):
    lefts, values, rest = rest[:count], rest[count : count + groups], rest[count + groups :]
    refs, (left, right, whole) = rest[: len(shares)], rest[len(shares) :]
    tall = groups * HEAD_DIM + 16
    for item in range(count):
        left[pl.ds(item * tall, tall), :] = lefts[item][0]
        for k in range(groups):
            block = values[k][item]
            right[pl.ds(item * tall + k * HEAD_DIM, HEAD_DIM), :] = jnp.where(
                keep_of(lengths, item * groups + k), block, jnp.zeros_like(block)
            )
        right[pl.ds(item * tall + groups * HEAD_DIM, 16), :] = reach(
            lengths, item * groups, groups
        ).astype(bf16)
    whole[...] = times(left[...].T, right[...]).astype(bf16)
    at = 0
    for ref, (number, rows) in zip(refs, shares):
        for k in range(number):
            ref[k, 0] = whole[pl.ds(pl.multiple_of(offsets[at], rows), rows), :]
            at += 1


def logits_back(lengths, offsets, lefts, values, shares, after=()):
    count, groups = len(lefts), len(values)
    heads, tall, _ = lefts[0].shape
    block = pl.BlockSpec((count, HEAD_DIM, LENGTH), lambda h, *_: (0, h, 0))
    return call(
        functools.partial(logits_back_kernel, count=count, groups=groups, shares=shares),
        "logits_back",
        (heads,),
        [lengths, offsets],
        [(v, pl.BlockSpec((1, tall, LENGTH), lambda h, *_: (h, 0, 0))) for v in lefts]
        + [(v, block) for v in values],
        [
            (
                shape(number, heads, rows, LENGTH),
                pl.BlockSpec((number, 1, rows, LENGTH), lambda h, *_: (0, h, 0, 0)),
            )
            for number, rows in shares
        ],
        [
            pltpu.VMEM((count * tall, LENGTH), bf16),
            pltpu.VMEM((count * tall, LENGTH), bf16),
            pltpu.VMEM((LENGTH, LENGTH), bf16),
        ],
        2 * heads * count * tall * LENGTH * LENGTH,
        14 << 20,
        after,
    )


def load_weight(offsets, pieces, held, sem):
    copies = []
    at = 0
    for piece in pieces:
        count, rows, columns = piece.shape
        for k in range(count):
            start = pl.multiple_of(offsets[2 * at], 16)
            side = pl.multiple_of(offsets[2 * at + 1], 128)
            copies.append(
                pltpu.make_async_copy(
                    piece.at[k], held.at[pl.ds(start, rows), pl.ds(side, columns)], sem.at[at]
                )
            )
            at += 1
    for copy in copies:
        copy.start()
    for copy in copies:
        copy.wait()


def halves(total, gain, low, high):
    half = WIDTH // 2
    column = jnp.broadcast_to(gain, (128, WIDTH)).T
    leading = column.astype(bf16)
    low[:, pl.ds(0, half)] = total[:, :half].astype(bf16)
    high[:, pl.ds(0, half)] = total[:, half:].astype(bf16)
    low[:, pl.ds(half, 128)] = leading
    high[:, pl.ds(half, 128)] = (column - leading.astype(f32)).astype(bf16)


class Refs:
    def __init__(self, refs):
        self.refs, self.at = refs, 0

    def take(self, count=None):
        if count is None:
            self.at += 1
            return self.refs[self.at - 1]
        self.at += count
        return self.refs[self.at - count : self.at]


def feed_kernel(where, units_at, *refs, first, last, carried, settled, plain, slices, groups, parts):
    refs = Refs(refs)
    grad_ref, weights = refs.take(), refs.take()
    mixed = refs.take(groups) if first or last else None
    w_ref = refs.take() if last and not first else None
    if first:
        x_ref = refs.take()
    else:
        hidden_ref, scaled_ref, out_ref, back_ref = refs.take(4)
    if carried:
        carry = refs.take(2 + 2 * last)
    if last and carried:
        refs.take()
    if first:
        hidden_out, scaled_out, w_out = refs.take(3)
    if last:
        result_ref, grad_hidden_ref, grads = refs.take(), refs.take(), refs.take(groups)
    else:
        out_next, back_next = refs.take(2)
    if settled and plain:
        joint = refs.take(1 + last)
    elif settled:
        keeps, sends = refs.take(parts[0]), refs.take(parts[1])
        if last:
            w_keeps, w_sends = refs.take(parts[0]), refs.take(parts[1])
    else:
        handed = refs.take(2 + 2 * last)
    held, active, grad_pre, sum_up, sum_down, sems, loaded = refs.take(7)
    brought = refs.take(2 + 2 * last) if carried else ()
    if first or last:
        turned = refs.take()
    if last:
        scratch, sum_w, sum_gain, low, high = refs.take(5)
    step = pl.program_id(0)
    final = step == pl.num_programs(0) - 1
    units = slices * WIDTH
    up_ref = held.at[:, pl.ds(0, units)]
    down_ref = held.at[:, pl.ds(units, units)]
    downs = [held.at[:, pl.ds(units + q * WIDTH, WIDTH)] for q in range(slices)]
    if first:
        w_ref = held.at[:, pl.ds(2 * units, WIDTH)]
    sums = [sum_up, sum_down] + ([sum_w, sum_gain] if last else [])

    def bring():
        return [pltpu.make_async_copy(carry[k], brought[k], sems.at[k]) for k in range(len(brought))]

    def load(at):
        side = pl.ds(at * units, WIDTH if at == 2 else units)
        return pltpu.make_async_copy(weights.at[0, :, side], held.at[:, side], loaded.at[at])

    @pl.when(step == 0)
    def _():
        for at in (2, 0, 1) if first else (0, 1):
            load(at).start()
        for copy in bring():
            copy.start()
        for total in sums:
            total[...] = jnp.zeros_like(total)
        if first:
            load(2).wait()
            w_out[...] = w_ref[...]

    if first or last:
        spread(turned, mixed, where[0])
    if first:
        hidden = x_ref[0].astype(f32) + times(turned[...].T, w_ref[...])
        hidden_out[...] = hidden
        scaled = (hidden * rms(hidden)).astype(bf16)
        scaled_out[...] = scaled
    else:
        scaled = scaled_ref[...]

    @pl.when(step == 0)
    def _():
        load(0).wait()
        load(1).wait()

    grad = grad_ref[0]
    slab = 256
    for k in range(units // slab):
        at = pl.ds(k * slab, slab)
        inner = pl.ds(k * slab % WIDTH, slab)
        pre = turned_by_rows(up_ref[:, at], scaled)
        grad_active = rows_by_rows(downs[k * slab // WIDTH][inner, :], grad)
        square = pre * pre
        half = 0.5 + 0.5 * jnp.tanh(pre * (FIRST + SECOND * square))
        act = pre * half
        active[at, :] = act.astype(bf16)
        slope = half + act * (1.0 - half) * (2.0 * FIRST + 6.0 * SECOND * square)
        grad_pre[at, :] = (grad_active * slope).astype(bf16)
    out = sum(
        turned_times(downs[q][...], active[pl.ds(q * WIDTH, WIDTH), :]) for q in range(slices)
    )
    back = times(up_ref[...], grad_pre[...])
    if not first:
        out, back = out + out_ref[...], back + back_ref[...]
    for q in range(slices):
        at = pl.ds(q * WIDTH, WIDTH)
        sum_down[at, :] += times(active[at, :], grad)
        sum_up[at, :] += times(grad_pre[at, :], scaled)
    if last:
        hidden = hidden if first else hidden_ref[...]
        result_ref[0] = (hidden + out.T).astype(bf16)
        weighted = back.T
        scale = rms(hidden)
        both = weighted * hidden
        mean = jnp.mean(both, axis=-1, keepdims=True)
        attended = (grad.astype(f32) + scale * weighted - hidden * (scale**3 * mean)).astype(bf16)
        grad_hidden_ref[...] = attended
        scratch[...] = rows_by_rows(w_ref[...], attended).astype(bf16)
        pick(scratch, grads, where[0])
        sum_w[...] += times(turned[...], attended)
        sum_gain[...] += jnp.sum(both * scale, axis=0, keepdims=True)
    else:
        out_next[...] = out
        back_next[...] = back

    @pl.when(final)
    def _():
        for copy in bring():
            copy.wait()
        for total, more in zip(sums, brought):
            total[...] += more[...].astype(f32)
        if settled:
            for q in range(slices):
                at = pl.ds(q * WIDTH, WIDTH)
                up_ref[:, at] = sum_up[at, :].T.astype(bf16)
                down_ref[:, at] = sum_down[at, :].astype(bf16)
            if last:
                halves(sum_w[...], sum_gain[...], low, high)
            if plain:
                joint[0][...] = held[:, pl.ds(0, 2 * units)]
                if last:
                    joint[1][:, pl.ds(0, low.shape[1])] = low[...]
                    joint[1][:, pl.ds(low.shape[1], low.shape[1])] = high[...]
            else:
                share_two(where[2], units_at, 0, keeps, sends, up_ref, down_ref)
                if last:
                    share_two(where[2], units_at, 0, w_keeps, w_sends, low, high)
        else:
            for total, ref in zip(sums, handed):
                ref[...] = total[...].astype(ref.dtype)


def feed(where, units_at, item, chunk, grad, packed, w_out, tokens, mixed, state, carry, earlier, shapes, settled, after=()):
    rows = 256
    groups, parts, plain = len(mixed), [len(kind) for kind in shapes or ()], shapes is None
    group = mixed[0].shape[0]
    first, last = chunk == 0, chunk == CHUNKS - 1
    slices = HIDDEN // CHUNKS // WIDTH
    units = slices * WIDTH
    once = pl.Buffered(1)
    tall = pl.BlockSpec((1, rows, WIDTH), lambda j, *_: (item, j, 0))
    flat = pl.BlockSpec((rows, WIDTH), lambda j, *_: (j, 0))
    wide = pl.BlockSpec((WIDTH, rows), lambda j, *_: (0, j))
    split = pl.BlockSpec((group, rows), lambda j, *_: (0, j))
    square = pl.BlockSpec((WIDTH, WIDTH), lambda j, *_: (0, 0), pipeline_mode=once)
    operands = [(grad, tall), (packed, ANY)]
    if first or last:
        operands += [(m, split) for m in mixed]
    if last and not first:
        operands += [(w_out, square)]
    if first:
        operands += [(tokens, tall)]
    else:
        operands += list(zip(state, (flat, flat, wide, wide)))
    aliases = {}
    if carry:
        operands += [(c, ANY) for c in carry]
    outputs = []
    if first:
        outputs += [(shape(LENGTH, WIDTH, kind=f32), flat), (shape(LENGTH, WIDTH), flat), (shape(WIDTH, WIDTH), square)]
    if last:
        if carry:
            aliases = {2 + len(operands): len(outputs)}
            operands += [(e, ANY) for e in earlier]
        outputs += [(shape(*grad.shape), tall), (shape(LENGTH, WIDTH), flat)]
        outputs += [(shape(group, LENGTH), split)] * groups
    else:
        outputs += [(shape(WIDTH, LENGTH, kind=f32), wide)] * 2
    fixed = len(outputs)
    handed = [shape(units, WIDTH)] * 2
    if last:
        handed += [shape(WIDTH, WIDTH), shape(1, WIDTH, kind=f32)]
    if settled:
        if plain:
            sizes = [shape(WIDTH, 2 * units), shape(WIDTH, WIDTH + 256)][: 1 + last]
        else:
            sizes = [shape(c, r, units) for kind in shapes for c, r in kind]
            if last:
                sizes += [shape(c, r, WIDTH // 2 + 128) for kind in shapes for c, r in kind]
        outputs += [
            (u, pl.BlockSpec(u.shape, lambda j, *_, n=len(u.shape): (0,) * n, pipeline_mode=once))
            for u in sizes
        ]
    else:
        sizes = handed
        outputs += [(u, pl.BlockSpec(u.shape, lambda j, *_: (0, 0), pipeline_mode=once)) for u in sizes]
    scratch = [
        pltpu.VMEM((WIDTH, 2 * units + WIDTH * first), bf16),
        pltpu.VMEM((units, rows), bf16),
        pltpu.VMEM((units, rows), bf16),
        pltpu.VMEM((units, WIDTH), f32),
        pltpu.VMEM((units, WIDTH), f32),
        pltpu.SemaphoreType.DMA((4,)),
        pltpu.SemaphoreType.DMA((3,)),
    ]
    if carry:
        scratch += [pltpu.VMEM(u.shape, u.dtype) for u in handed]
    if first or last:
        scratch += [pltpu.VMEM((WIDTH, rows), bf16)]
    if last:
        scratch += [
            pltpu.VMEM((WIDTH, rows), bf16),
            pltpu.VMEM((WIDTH, WIDTH), f32),
            pltpu.VMEM((1, WIDTH), f32),
            pltpu.VMEM((WIDTH, WIDTH // 2 + 128), bf16),
            pltpu.VMEM((WIDTH, WIDTH // 2 + 128), bf16),
        ]
    outs = call(
        functools.partial(
            feed_kernel,
            first=first,
            last=last,
            carried=bool(carry),
            settled=settled,
            plain=plain,
            slices=slices,
            groups=groups,
            parts=parts,
        ),
        "feed",
        (LENGTH // rows,),
        [where, units_at],
        operands,
        outputs,
        scratch,
        12 * LENGTH * WIDTH * units,
        20 << 20,
        after,
        aliases,
    )
    main, sums = outs[:fixed], outs[fixed:]
    if settled and not plain:
        keep, both = parts[0], sum(parts)
        sums = [(sums[at : at + keep], sums[at + keep : at + both]) for at in range(0, len(sums), both)]
    return main, sums


def tokens_kernel(where, units_at, *refs, groups, parts, carried, settled, plain):
    refs = Refs(refs)
    x_ref, grad_ref, w_ref, grads = refs.take(), refs.take(), refs.take(), refs.take(groups)
    if carried:
        carry = refs.take(2)
        refs.take()
    result_ref = refs.take()
    if settled and plain:
        joint = refs.take()
    elif settled:
        keeps, sends = refs.take(parts[0]), refs.take(parts[1])
    else:
        handed = refs.take(2)
    turned, sum_w, sum_gain, low, high, sems = refs.take(6)
    brought = refs.take(2) if carried else ()
    step = pl.program_id(0)
    sums = [sum_w, sum_gain]

    def bring():
        return [pltpu.make_async_copy(carry[k], brought[k], sems.at[k]) for k in range(2)] if carried else []

    @pl.when(step == 0)
    def _():
        for copy in bring():
            copy.start()
        for total in sums:
            total[...] = jnp.zeros_like(total)

    spread(turned, grads, where[0])
    x = x_ref[0].astype(f32)
    scale = rms(x)
    scaled = (x * scale).astype(bf16)
    weighted = rows_by_rows(turned[...].T, w_ref[...])
    both = weighted * x
    mean = jnp.mean(both, axis=-1, keepdims=True)
    total = grad_ref[...].astype(f32) + scale * weighted - x * (scale**3 * mean)
    result_ref[0] = total.astype(bf16)
    sum_gain[...] += jnp.sum(both * scale, axis=0, keepdims=True)
    sum_w[...] += times(turned[...], scaled)

    @pl.when(step == pl.num_programs(0) - 1)
    def _():
        for copy in bring():
            copy.wait()
        for total, more in zip(sums, brought):
            total[...] += more[...]
        if settled:
            halves(sum_w[...].T, sum_gain[...], low, high)
            if plain:
                joint[:, pl.ds(0, low.shape[1])] = low[...]
                joint[:, pl.ds(low.shape[1], low.shape[1])] = high[...]
            else:
                share_two(where[2], units_at, 0, keeps, sends, low, high)
        else:
            copies = [pltpu.make_async_copy(sums[k], handed[k], sems.at[k]) for k in range(2)]
            for copy in copies:
                copy.start()
            for copy in copies:
                copy.wait()


def grad_tokens_of(where, units_at, item, tokens, grad_hidden, weight, grads, carry, earlier, shapes, settled, after=()):
    rows = 256
    groups, parts, plain = len(grads), [len(kind) for kind in shapes or ()], shapes is None
    group = grads[0].shape[0]
    tall = pl.BlockSpec((1, rows, WIDTH), lambda j, *_: (item, j, 0))
    whole = lambda j, *_: (0, 0)
    operands = [
        (tokens, tall),
        (grad_hidden, pl.BlockSpec((rows, WIDTH), lambda j, *_: (j, 0))),
        (weight, pl.BlockSpec((WIDTH, WIDTH), whole)),
    ] + [(g, pl.BlockSpec((group, rows), lambda j, *_: (0, j))) for g in grads]
    aliases = {}
    if carry:
        operands += [(c, ANY) for c in carry]
        aliases = {2 + len(operands): 0}
        operands += [(earlier, ANY)]
    outputs = [(shape(*tokens.shape), tall)]
    half = WIDTH // 2 + 128
    if settled:
        sizes = [shape(c, r, half) for kind in shapes or () for c, r in kind]
        outputs += [(u, pl.BlockSpec(u.shape, lambda j, *_: (0, 0, 0))) for u in sizes]
        if plain:
            outputs += [(shape(WIDTH, 2 * half), pl.BlockSpec((WIDTH, 2 * half), whole))]
    else:
        outputs += [(shape(WIDTH, WIDTH, kind=f32), ANY), (shape(1, WIDTH, kind=f32), ANY)]
    outs = call(
        functools.partial(tokens_kernel, groups=groups, parts=parts, carried=bool(carry), settled=settled, plain=plain),
        "grad_tokens",
        (LENGTH // rows,),
        [where, units_at],
        operands,
        outputs,
        [
            pltpu.VMEM((WIDTH, rows), bf16),
            pltpu.VMEM((WIDTH, WIDTH), f32),
            pltpu.VMEM((1, WIDTH), f32),
            pltpu.VMEM((WIDTH, half), bf16),
            pltpu.VMEM((WIDTH, half), bf16),
            pltpu.SemaphoreType.DMA((2,)),
        ]
        + [pltpu.VMEM((WIDTH, WIDTH), f32), pltpu.VMEM((1, WIDTH), f32)][: 2 * bool(carry)],
        4 * LENGTH * WIDTH * WIDTH,
        8 << 20,
        after,
        aliases,
    )
    if settled and not plain:
        return outs[0], (outs[1 : 1 + parts[0]], outs[1 + parts[0] :])
    return outs[0], outs[1:]


def halved(array):
    half = array.shape[1] // 2
    return array[:, :half], array[:, half:]


def hold(*values):
    return lax.optimization_barrier(values)


def exchange(parts):
    got = [parts[0]]
    for r in range(1, len(parts)):
        got.append(lax.ppermute(parts[r], "dp", [(i, i ^ r) for i in range(len(parts))]))
    return got


def add(*terms):
    return functools.reduce(jnp.add, [t.astype(f32) for t in terms]).astype(bf16)


class Chips:
    def __init__(self, groups, seqs):
        self.groups, self.seqs, self.rings = groups, seqs, seqs // 2
        self.here, self.row = lax.axis_index("dp"), lax.axis_index("seq")
        self.core, self.z = self.row % 2, self.row // 2

    def across(self, array):
        return lax.ppermute(array, "seq", [(i, i ^ 1) for i in range(self.seqs)])

    def along(self, array, step):
        n = self.seqs
        return lax.ppermute(array, "seq", [(i, (i + 2 * step) % n) for i in range(n)])

    def over(self, array, bits):
        return lax.ppermute(array, "dp", [(i, i ^ bits) for i in range(self.groups)])

    def hop(self, array, step):
        return lax.ppermute(array, "seq", [(i, i ^ (2 * step)) for i in range(self.seqs)])

    def chip(self, bits, step):
        return (self.here ^ bits) * self.rings + (self.z ^ step)

    def chips(self):
        return [self.chip(b, s) for b in range(self.groups) for s in range(self.rings)]

    def gather_line(self, mine):
        return jnp.stack([mine] + [self.hop(mine, s) for s in range(1, self.rings)])

    def gather_plane(self, ring):
        return [ring] + [self.over(ring, bits) for bits in range(1, self.groups)]

    def gathered_at(self, rows):
        return jnp.stack([v for c in self.chips() for v in (c * rows, 0 * c)]).astype(jnp.int32)

    def unit_order(self, rows):
        return jnp.stack([c * rows for c in self.chips()]).astype(jnp.int32)

    def scatter_core(self, shares):
        keeps, (send,) = shares
        got, n = self.across(send), self.rings
        return [add(keep, got[b * n : (b + 1) * n]) for b, keep in enumerate(keeps)]

    def scatter_plane(self, parts):
        return self.join_plane([parts[0]] + [self.over(parts[b], b) for b in range(1, self.groups)])

    def join_plane(self, parts):
        return [add(*[part[s] for part in parts]) for s in range(self.rings)]

    def scatter_line(self, own):
        return add(own[0], *[self.hop(own[s], s) for s in range(1, self.rings)])

    def settle(self, total):
        rows = total.shape[0] // 2
        mine = lax.dynamic_slice_in_dim(total, self.core * rows, rows)
        other = self.across(lax.dynamic_slice_in_dim(total, (1 - self.core) * rows, rows))
        first = self.core == 0
        return jnp.where(first, mine, other), jnp.where(first, other, mine)


def body(tokens, lengths, mixer, gain_one, gain_two, w_value, w_out, w_up, w_down, cotangent, groups, seqs):
    ranks = groups * seqs
    fast = groups == 4 and seqs == 8
    chips = Chips(groups, seqs)
    here, row, core = chips.here, chips.row, chips.core
    where = jnp.stack([here, row, core]).astype(jnp.int32)
    items = tokens.shape[0]
    shard = w_value.shape[0]
    slices = HIDDEN // WIDTH
    width = slices // CHUNKS
    half = WIDTH // 2

    first_gain = gain_one.astype(f32)[:, None]
    second_gain = gain_two.astype(f32)[:, None]
    value_mine = (w_value.astype(f32) * first_gain).astype(bf16)
    up_mine = (w_up.astype(f32) * second_gain).astype(bf16)
    up_mine = up_mine.reshape(shard, ranks, slices, shard).swapaxes(1, 2)
    down_mine = w_down.reshape(slices, shard, WIDTH).swapaxes(0, 1)
    weights = [value_mine]
    for chunk in range(CHUNKS):
        at = slice(chunk * width, (chunk + 1) * width)
        columns = [m[:, at].reshape(shard, width * WIDTH) for m in (up_mine, down_mine)]
        weights.append(jnp.concatenate(columns + [w_out][chunk:], axis=1))

    logits = jnp.exp(mixer.astype(f32))
    logits_low = logits.astype(bf16)
    block = logits.shape[1]
    shares_at, shares = [0], ((1, LENGTH),)
    early = weights[1:2] if fast else weights
    whole = [lax.all_gather(w, ALL, axis=0, tiled=True)[None] for w in early]
    weights_at = [jnp.zeros((2,), jnp.int32)] * (1 + CHUNKS)
    if fast:
        rings = chips.rings
        whole = [None] + whole
        other = chips.across(value_mine)
        value_unit = jnp.where(
            core == 0, jnp.concatenate([value_mine, other]), jnp.concatenate([other, value_mine])
        )
        weights_at[0] = chips.gathered_at(2 * shard)
        zs = [(chips.z - s) % rings for s in (0, 1, 3, 2)]
        logits_at = [(2 * z + c) * block for c in (core, 1 - core) for z in zs]
        shapes = (((rings, 2 * shard),) * groups, ((groups * rings, 2 * shard),))
        order = chips.unit_order(2 * shard)
    else:
        value_parts = whole[:1]
        logits_parts = [lax.all_gather(logits_low, "seq", axis=1, tiled=True)]
        logits_at = [0]
        shapes = None
        order = jnp.zeros((1,), jnp.int32)
    logits_at, shares_at = (
        jnp.stack([jnp.asarray(v, jnp.int32) for v in at]) for at in (logits_at, shares_at)
    )
    def fed(pairs):
        ups, downs = (jnp.concatenate(parts, axis=1).astype(f32) for parts in zip(*pairs))
        sum_up = ups.reshape(shard, slices, ranks, shard).swapaxes(1, 2).reshape(shard, HIDDEN)
        sum_down = downs.reshape(shard, slices, WIDTH).swapaxes(0, 1)
        return sum_up * second_gain, sum_down.reshape(shard * slices, WIDTH)

    def joined(pair):
        low, high = (part.astype(f32) for part in pair)
        return jnp.concatenate([low[:, :half], high[:, :half]], axis=1), low[:, half] + high[:, half]

    def lengths_of():
        return jnp.stack(exchange([lengths] * groups), axis=1).reshape(-1)

    def values_of(after=()):
        return project_values(where, weights_at[0], tokens, value_parts, groups, after)

    def mix(item, values, after=()):
        return mix_items(lengths_here, logits_at, values, logits_parts, item, after)

    def run_feed(item, chunk, packed, w_out_all, mixed, state, carry, result, after=()):
        return feed(
            where, order, item, chunk, cotangent, packed, w_out_all, tokens,
            mixed, state, carry, (result,), shapes if chunk else None, item == items - 1, after,
        )

    def back(item, grads, mixed_out, sums, after=()):
        return values_back(
            lengths_here, logits_at, grads, mixed_out, sums, logits_parts, item * groups, after
        )

    def close(item, grad_hidden, grads, carry, earlier, after=()):
        return grad_tokens_of(
            where, order, item, tokens, grad_hidden, value_all, grads, carry, earlier, shapes,
            item == items - 1, after,
        )

    if fast:
        assert items == 2 and CHUNKS == 2
        value_ring = chips.gather_line(value_unit)
        value_ring, logits_low, second, lengths_here = hold(
            value_ring, logits_low, weights[2], lengths_of()
        )
        value_parts = chips.gather_plane(value_ring)
        next_one, last_one = chips.along(logits_low, 1), chips.along(logits_low, 3)
        values, value_all = values_of()
        values = exchange(values)
        next_two = chips.along(next_one, 1)
        values, logits_low = hold(values, logits_low)
        next_two, last_one, values = hold(next_two, last_one, values)
        logits_parts = [logits_low, next_one, last_one, next_two]
        logits_parts += [chips.across(r) for r in logits_parts]
        mixed_out_a, sums_a = mix(0, values)
        mixed_out_a, sums_a, second = hold(mixed_out_a, sums_a, second)
        second = lax.all_gather(second, ALL, axis=0, tiled=True)
        mixed_a = exchange(mixed_out_a)
        mixed_out_b, sums_b = mix(1, values)
        mixed_out_b, mixed_a = hold(mixed_out_b, mixed_a)
        mixed_b = exchange(mixed_out_b)
        first = whole[1]
        state_a, carry = run_feed(0, 0, first, None, mixed_a, None, (), None)
        state_a, carry, mixed_b = hold(state_a, carry, mixed_b)
        w_out_all = state_a[2]
        state_b, (shared,) = run_feed(1, 0, first, None, mixed_b, None, carry, None)
        first_sums = lax.psum_scatter(shared, ALL, scatter_dimension=0, tiled=True)
        state_a = state_a[:2] + state_a[3:]
        state_b = state_b[:2] + state_b[3:]
        second = second[None]
        out_a, carry = run_feed(0, 1, second, w_out_all, mixed_a, state_a, (), None)
        out_a, carry = hold(out_a, carry)
        grads_a = exchange(out_a[2:])
        out_b, (second_shared, out_shared) = run_feed(
            1, 1, second, w_out_all, mixed_b, state_b, carry, out_a[0]
        )
        out_b, grads_a, second_shared, out_shared = hold(out_b, grads_a, second_shared, out_shared)
        result = out_b[0]
        grads_b = exchange(out_b[2:])
        back_a, left_a = back(0, grads_a, mixed_out_a, sums_a)
        back_a, left_a, grads_b, second_shared, out_shared = hold(
            back_a, left_a, grads_b, second_shared, out_shared
        )
        back_a = exchange(back_a)
        back_b, left_b = back(1, grads_b, mixed_out_b, sums_b)
        second_sums, out_sums = chips.scatter_core(second_shared), chips.scatter_core(out_shared)
        second_sums = [jnp.concatenate(pair, axis=2) for pair in zip(second_sums, out_sums)]
        back_b, left_b, second_sums = hold(back_b, left_b, second_sums)
        back_b = exchange(back_b)
        grad_logits = logits_back(lengths_here, shares_at, [left_a, left_b], values, shares)
        grad_logits, back_a, second_sums = hold(grad_logits, back_a, second_sums)
        grad_mixer = lax.psum_scatter(grad_logits[0][0], "seq", scatter_dimension=1, tiled=True)
        grad_tokens, carry = close(0, out_a[1], back_a, (), None)
        carry, back_b, grad_tokens, second_sums = hold(carry, back_b, grad_tokens, second_sums)
        second_plane = [chips.over(second_sums[b], b) for b in range(1, groups)]
        grad_tokens, shared = close(1, out_b[1], back_b, carry, grad_tokens)
        shared, second_plane[:2] = hold(shared, second_plane[:2])
        value_sums = chips.scatter_core(shared)
        value_sums, second_plane[2:] = hold(value_sums, second_plane[2:])
        second_sums = chips.join_plane([second_sums[0]] + list(second_plane))
        second_line = [chips.hop(second_sums[k], k) for k in range(1, rings)]
        value_sums = chips.scatter_plane(value_sums)
        value_sums, second_line = hold(value_sums, second_line)
        value_line = [chips.hop(value_sums[k], k) for k in range(1, rings)]
        second_sums = chips.settle(add(second_sums[0], *second_line))
        wide = width * WIDTH
        sum_up, sum_down = fed([halved(first_sums), tuple(part[:, :wide] for part in second_sums)])
        sum_out, gain_two_sum = joined([part[:, wide:] for part in second_sums])
        grad_mixer = grad_mixer.astype(f32) * logits
        value_line, grad_mixer, sum_up, sum_down, sum_out, gain_two_sum = hold(
            value_line, grad_mixer, sum_up, sum_down, sum_out, gain_two_sum
        )
        settled = [chips.settle(add(value_sums[0], *value_line))]
    else:
        lengths_here = lengths_of()
        values, value_all = values_of()
        values = exchange(values)
        mixed_out, sums, mixed = [], [], []
        for item in range(items):
            out, total = mix(item, values)
            mixed_out.append(out)
            sums.append(total)
            mixed.append(exchange(out))
        states, w_out_all, result = [None] * items, None, None
        grads, grad_hidden, shared = [None] * items, [None] * items, []
        for chunk in range(CHUNKS):
            carry = ()
            for item in range(items):
                state, carry = run_feed(
                    item, chunk, whole[1 + chunk], w_out_all, mixed[item], states[item], carry, result
                )
                if chunk == CHUNKS - 1:
                    result, grad_hidden[item], grads[item] = state[0], state[1], exchange(state[2:])
                elif chunk == 0:
                    if item == items - 1:
                        w_out_all = state[2]
                    states[item] = list(state[:2]) + list(state[3:])
                else:
                    states[item] = list(states[item][:2]) + list(state)
            shared += carry
        lefts, grad_values = [], []
        for item in range(items):
            out, left = back(item, grads[item], mixed_out[item], sums[item])
            lefts.append(left)
            grad_values.append(exchange(out))
        grad_logits = logits_back(lengths_here, shares_at, lefts, values, shares)
        carry, grad_tokens = (), None
        for item in range(items):
            grad_tokens, carry = close(item, grad_hidden[item], grad_values[item], carry, grad_tokens)
        shared += carry
        grad_mixer = lax.psum_scatter(grad_logits[0][0], "seq", scatter_dimension=1, tiled=True)
        settled = [halved(lax.psum_scatter(x, ALL, scatter_dimension=0, tiled=True)) for x in shared]
    if not fast:
        sum_up, sum_down = fed(settled[:CHUNKS])
        sum_out, gain_two_sum = joined(settled[CHUNKS])
        grad_mixer = grad_mixer.astype(f32) * logits
    sum_value, gain_one_sum = joined(settled[-1])
    return (
        result,
        grad_tokens,
        grad_mixer,
        gain_one_sum / first_gain[:, 0],
        gain_two_sum / second_gain[:, 0],
        sum_value * first_gain,
        sum_out,
        sum_up,
        sum_down,
    )


def solution(mesh):
    rows = P(ALL, None)
    line = P(ALL)
    cube = P(ALL, None, None)
    logits = P("dp", "seq", None)
    return jax.shard_map(
        functools.partial(body, groups=mesh.shape["dp"], seqs=mesh.shape["seq"]),
        mesh=mesh,
        in_specs=(cube, line, logits, line, line, rows, rows, rows, rows, cube),
        out_specs=(cube, cube, logits, line, line, rows, rows, rows, rows),
        check_vma=False,
    )
```

```python
import functools

import jax
import jax.numpy as jnp
from jax import lax
from jax.experimental import pallas as pl
from jax.experimental.pallas import tpu as pltpu
from jax.sharding import PartitionSpec as P

epsilon = 1e-06
bf16 = jnp.bfloat16
f32 = jnp.float32
WIDTH = 768
LENGTH = 1024
HIDDEN = 3072
HEADS = 12
HEAD_DIM = 64
CHUNKS = 2


def rows_by_rows(left, right):
    return lax.dot_general(left, right, (((1,), (1,)), ((), ())), preferred_element_type=f32)


def turned_by_rows(left, right):
    return lax.dot_general(left, right, (((0,), (1,)), ((), ())), preferred_element_type=f32)


def turned_times(left, right):
    return lax.dot_general(left, right, (((0,), (0,)), ((), ())), preferred_element_type=f32)


def times(left, right):
    return jnp.dot(left, right, preferred_element_type=f32)


def rms(values):
    return lax.rsqrt(jnp.mean(values * values, axis=-1, keepdims=True) + epsilon)


def share(offsets, at, refs, source):
    for ref in refs:
        count, rows, _ = ref.shape
        for k in range(count):
            ref[k] = source[pl.ds(pl.multiple_of(offsets[at], 16), rows), :]
            at += 1
    return at


def share_two(core, offsets, at, keeps, sends, first, second):
    @pl.when(core == 0)
    def _():
        share(offsets, at, keeps, first)
        share(offsets, at, sends, second)

    @pl.when(core != 0)
    def _():
        share(offsets, at, keeps, second)
        share(offsets, at, sends, first)


VMEM = 59 * 1024 * 1024
SCALE = 0.001
ANY = pl.BlockSpec(memory_space=pl.ANY)
ALL = ("dp", "seq")
FIRST = 0.7978845608028654
SECOND = FIRST * 0.044715


def call(kernel, name, grid, scalars, operands, outputs, scratch, flops, moved, after=(), aliases=None):
    count = len(scalars) + len(operands)

    def run(*refs):
        kernel(*refs[:count], *refs[count + len(after) :])

    return pl.pallas_call(
        run,
        grid_spec=pltpu.PrefetchScalarGridSpec(
            num_scalar_prefetch=len(scalars),
            grid=grid,
            in_specs=[block for _, block in operands] + [ANY] * len(after),
            out_specs=[block for _, block in outputs],
            scratch_shapes=scratch,
        ),
        out_shape=[shape for shape, _ in outputs],
        input_output_aliases=aliases or {},
        compiler_params=pltpu.CompilerParams(vmem_limit_bytes=VMEM),
        cost_estimate=pl.CostEstimate(
            flops=int(flops * SCALE), bytes_accessed=int(moved * SCALE), transcendentals=0
        ),
        name=name,
    )(*scalars, *[array for array, _ in operands], *after)


def shape(*sizes, kind=bf16):
    return jax.ShapeDtypeStruct(sizes, kind)


def spread(scratch, refs, place):
    for at, ref in enumerate(refs):
        group = ref.shape[0]
        scratch[pl.ds(pl.multiple_of((place ^ at) * group, 64), group), :] = ref[...]


def pick(scratch, refs, place):
    for at, ref in enumerate(refs):
        group = ref.shape[0]
        ref[...] = scratch[pl.ds(pl.multiple_of((place ^ at) * group, 64), group), :]


def values_kernel(where, offsets, x_ref, *rest, pieces, groups):
    parts, rest = rest[:pieces], rest[pieces:]
    outs, (w_ref, turned, scratch, sem) = rest[:groups], rest[groups:]
    step = pl.program_id(0)

    @pl.when(step == 0)
    def _():
        load_weight(offsets, parts, w_ref, sem)
        turned[...] = w_ref[...].T

    for half in range(2):
        at = pl.ds(half * LENGTH // 2, LENGTH // 2)
        x = x_ref[0, at, :].astype(f32)
        scaled = (x * rms(x)).astype(bf16)
        scratch[:, at] = rows_by_rows(turned[...], scaled).astype(bf16)
    pick(scratch, [out.at[0] for out in outs], where[0])


def project_values(where, offsets, tokens, parts, groups, after):
    items = tokens.shape[0]
    group = WIDTH // groups
    units = sum(p.shape[0] for p in parts)
    whole = lambda *_: (0, 0)
    outs = call(
        functools.partial(values_kernel, pieces=len(parts), groups=groups),
        "project_values",
        (items,),
        [where, offsets],
        [(tokens, pl.BlockSpec((1, LENGTH, WIDTH), lambda i, *_: (i, 0, 0)))]
        + [(p, ANY) for p in parts],
        [(shape(items, group, LENGTH), pl.BlockSpec((1, group, LENGTH), lambda i, *_: (i, 0, 0)))] * groups
        + [(shape(WIDTH, WIDTH), pl.BlockSpec((WIDTH, WIDTH), whole))],
        [
            pltpu.VMEM((WIDTH, WIDTH), bf16),
            pltpu.VMEM((WIDTH, LENGTH), bf16),
            pltpu.SemaphoreType.DMA((units,)),
        ],
        2 * items * LENGTH * WIDTH * WIDTH,
        4 * items * LENGTH * WIDTH,
        after,
    )
    return outs[:groups], outs[groups]


def load_logits(offsets, pieces, held, sems):
    def copy(head, at):
        rows = pieces[at].shape[1]
        start = pl.multiple_of(offsets[at], rows)
        return pltpu.make_async_copy(
            pieces[at].at[head], held.at[head, pl.ds(start, rows)], sems.at[head, at]
        )

    head = pl.program_id(0)

    @pl.when(head == 0)
    def _():
        for h in range(held.shape[0]):
            for at in range(len(pieces)):
                copy(h, at).start()

    for at in range(len(pieces)):
        copy(head, at).wait()


def reach(lengths, base, count):
    which = lax.broadcasted_iota(jnp.int32, (16, LENGTH), 0)
    ends = jnp.zeros((16, LENGTH), jnp.int32)
    for k in range(count):
        ends = jnp.where(which == k, lengths[base + k], ends)
    return jnp.where(lax.broadcasted_iota(jnp.int32, (16, LENGTH), 1) < ends, 1.0, 0.0)


def keep_of(lengths, k):
    return lax.broadcasted_iota(jnp.int32, (1, LENGTH), 1) < lengths[k]


def mix_kernel(lengths, offsets, *rest, groups, pieces, base):
    values, parts = rest[:groups], rest[groups : groups + pieces]
    outs = rest[groups + pieces : 2 * groups + pieces]
    sums_ref, held, left, sems = rest[2 * groups + pieces :]
    load_logits(offsets, parts, held, sems)
    for k in range(groups):
        block = values[k][0]
        left[pl.ds(k * HEAD_DIM, HEAD_DIM), :] = jnp.where(
            keep_of(lengths, base + k), block, jnp.zeros_like(block)
        )
    left[pl.ds(groups * HEAD_DIM, 16), :] = reach(lengths, base, groups).astype(bf16)
    product = rows_by_rows(left[...], held[pl.program_id(0)])
    sums = product[groups * HEAD_DIM : groups * HEAD_DIM + 8]
    sums_ref[0] = sums
    for k in range(groups):
        mixed = product[k * HEAD_DIM : (k + 1) * HEAD_DIM] / sums[k : k + 1]
        outs[k][...] = jnp.where(keep_of(lengths, base + k), mixed, 0.0).astype(bf16)


def mix_items(lengths, offsets, values, parts, item, after=()):
    groups, pieces = len(values), len(parts)
    group = values[0].shape[1]
    base = item * groups
    heads = group // HEAD_DIM
    block = pl.BlockSpec((HEAD_DIM, LENGTH), lambda h, *_: (h, 0))
    outs = call(
        functools.partial(mix_kernel, groups=groups, pieces=pieces, base=base),
        "mix_items",
        (heads,),
        [lengths, offsets],
        [(v, pl.BlockSpec((1, HEAD_DIM, LENGTH), lambda h, *_: (item, h, 0))) for v in values] + [(p, ANY) for p in parts],
        [(shape(group, LENGTH), block)] * groups
        + [(shape(heads, 8, LENGTH, kind=f32), pl.BlockSpec((1, 8, LENGTH), lambda h, *_: (h, 0, 0)))],
        [
            pltpu.VMEM((heads, LENGTH, LENGTH), bf16),
            pltpu.VMEM((groups * HEAD_DIM + 16, LENGTH), bf16),
            pltpu.SemaphoreType.DMA((heads, pieces)),
        ],
        2 * heads * (groups * HEAD_DIM + 16) * LENGTH * LENGTH,
        12 << 20,
        after,
    )
    return outs[:groups], outs[groups]


def values_back_kernel(lengths, offsets, *rest, groups, pieces, base):
    grads, mixed, rest = rest[:groups], rest[groups : 2 * groups], rest[2 * groups :]
    sums_ref, parts = rest[0], rest[1 : 1 + pieces]
    outs = rest[1 + pieces : 1 + pieces + groups]
    left_ref, held, sems = rest[1 + pieces + groups :]
    load_logits(offsets, parts, held, sems)
    which = lax.broadcasted_iota(jnp.int32, (16, LENGTH), 0)
    extra = jnp.zeros((16, LENGTH), f32)
    for k in range(groups):
        keep = keep_of(lengths, base + k)
        inverse = jnp.where(keep, 1.0 / sums_ref[0, k : k + 1], 0.0)
        grad = grads[k][...].astype(f32)
        delta = jnp.sum(grad * mixed[k][...].astype(f32), axis=0, keepdims=True)
        left_ref[0, pl.ds(k * HEAD_DIM, HEAD_DIM), :] = (grad * inverse).astype(bf16)
        extra = jnp.where(which == k, -(delta * inverse), extra)
    left_ref[0, pl.ds(groups * HEAD_DIM, 16), :] = extra.astype(bf16)
    product = times(left_ref[0, pl.ds(0, groups * HEAD_DIM), :], held[pl.program_id(0)])
    for k in range(groups):
        part = product[k * HEAD_DIM : (k + 1) * HEAD_DIM]
        outs[k][...] = jnp.where(keep_of(lengths, base + k), part, 0.0).astype(bf16)


def values_back(lengths, offsets, grads, mixed, sums, parts, base, after=()):
    groups, pieces = len(grads), len(parts)
    group = grads[0].shape[0]
    heads = group // HEAD_DIM
    tall = groups * HEAD_DIM + 16
    block = pl.BlockSpec((HEAD_DIM, LENGTH), lambda h, *_: (h, 0))
    outs = call(
        functools.partial(values_back_kernel, groups=groups, pieces=pieces, base=base),
        "values_back",
        (heads,),
        [lengths, offsets],
        [(g, block) for g in grads]
        + [(m, block) for m in mixed]
        + [(sums, pl.BlockSpec((1, 8, LENGTH), lambda h, *_: (h, 0, 0)))]
        + [(p, ANY) for p in parts],
        [(shape(group, LENGTH), block)] * groups
        + [(shape(heads, tall, LENGTH), pl.BlockSpec((1, tall, LENGTH), lambda h, *_: (h, 0, 0)))],
        [
            pltpu.VMEM((heads, LENGTH, LENGTH), bf16),
            pltpu.SemaphoreType.DMA((heads, pieces)),
        ],
        2 * heads * tall * LENGTH * LENGTH,
        14 << 20,
        after,
    )
    return outs[:groups], outs[groups]


def logits_back_kernel(lengths, offsets, *rest, count, groups, shares):
    lefts, values, rest = rest[:count], rest[count : count + groups], rest[count + groups :]
    refs, (left, right, whole) = rest[: len(shares)], rest[len(shares) :]
    tall = groups * HEAD_DIM + 16
    for item in range(count):
        left[pl.ds(item * tall, tall), :] = lefts[item][0]
        for k in range(groups):
            block = values[k][item]
            right[pl.ds(item * tall + k * HEAD_DIM, HEAD_DIM), :] = jnp.where(
                keep_of(lengths, item * groups + k), block, jnp.zeros_like(block)
            )
        right[pl.ds(item * tall + groups * HEAD_DIM, 16), :] = reach(
            lengths, item * groups, groups
        ).astype(bf16)
    whole[...] = times(left[...].T, right[...]).astype(bf16)
    at = 0
    for ref, (number, rows) in zip(refs, shares):
        for k in range(number):
            ref[k, 0] = whole[pl.ds(pl.multiple_of(offsets[at], rows), rows), :]
            at += 1


def logits_back(lengths, offsets, lefts, values, shares, after=()):
    count, groups = len(lefts), len(values)
    heads, tall, _ = lefts[0].shape
    block = pl.BlockSpec((count, HEAD_DIM, LENGTH), lambda h, *_: (0, h, 0))
    return call(
        functools.partial(logits_back_kernel, count=count, groups=groups, shares=shares),
        "logits_back",
        (heads,),
        [lengths, offsets],
        [(v, pl.BlockSpec((1, tall, LENGTH), lambda h, *_: (h, 0, 0))) for v in lefts]
        + [(v, block) for v in values],
        [
            (
                shape(number, heads, rows, LENGTH),
                pl.BlockSpec((number, 1, rows, LENGTH), lambda h, *_: (0, h, 0, 0)),
            )
            for number, rows in shares
        ],
        [
            pltpu.VMEM((count * tall, LENGTH), bf16),
            pltpu.VMEM((count * tall, LENGTH), bf16),
            pltpu.VMEM((LENGTH, LENGTH), bf16),
        ],
        2 * heads * count * tall * LENGTH * LENGTH,
        14 << 20,
        after,
    )


def load_weight(offsets, pieces, held, sem):
    copies = []
    at = 0
    for piece in pieces:
        count, rows, columns = piece.shape
        for k in range(count):
            start = pl.multiple_of(offsets[2 * at], 16)
            side = pl.multiple_of(offsets[2 * at + 1], 128)
            copies.append(
                pltpu.make_async_copy(
                    piece.at[k], held.at[pl.ds(start, rows), pl.ds(side, columns)], sem.at[at]
                )
            )
            at += 1
    for copy in copies:
        copy.start()
    for copy in copies:
        copy.wait()


def halves(total, gain, low, high):
    half = WIDTH // 2
    column = jnp.broadcast_to(gain, (128, WIDTH)).T
    leading = column.astype(bf16)
    low[:, pl.ds(0, half)] = total[:, :half].astype(bf16)
    high[:, pl.ds(0, half)] = total[:, half:].astype(bf16)
    low[:, pl.ds(half, 128)] = leading
    high[:, pl.ds(half, 128)] = (column - leading.astype(f32)).astype(bf16)


class Refs:
    def __init__(self, refs):
        self.refs, self.at = refs, 0

    def take(self, count=None):
        if count is None:
            self.at += 1
            return self.refs[self.at - 1]
        self.at += count
        return self.refs[self.at - count : self.at]


def feed_kernel(where, units_at, *refs, first, last, carried, settled, plain, slices, groups, parts):
    refs = Refs(refs)
    grad_ref, weights = refs.take(), refs.take()
    mixed = refs.take(groups) if first or last else None
    w_ref = refs.take() if last and not first else None
    if first:
        x_ref = refs.take()
    else:
        hidden_ref, scaled_ref, out_ref, back_ref = refs.take(4)
    if carried:
        carry = refs.take(2 + 2 * last)
    if last and carried:
        refs.take()
    if first:
        hidden_out, scaled_out, w_out = refs.take(3)
    if last:
        result_ref, grad_hidden_ref, grads = refs.take(), refs.take(), refs.take(groups)
    else:
        out_next, back_next = refs.take(2)
    if settled and plain:
        joint = refs.take(1 + last)
    elif settled:
        keeps, sends = refs.take(parts[0]), refs.take(parts[1])
        if last:
            w_keeps, w_sends = refs.take(parts[0]), refs.take(parts[1])
    else:
        handed = refs.take(2 + 2 * last)
    held, active, grad_pre, sum_up, sum_down, sems, loaded = refs.take(7)
    brought = refs.take(2 + 2 * last) if carried else ()
    if first or last:
        turned = refs.take()
    if last:
        scratch, sum_w, sum_gain, low, high = refs.take(5)
    step = pl.program_id(0)
    final = step == pl.num_programs(0) - 1
    units = slices * WIDTH
    up_ref = held.at[:, pl.ds(0, units)]
    down_ref = held.at[:, pl.ds(units, units)]
    downs = [held.at[:, pl.ds(units + q * WIDTH, WIDTH)] for q in range(slices)]
    if first:
        w_ref = held.at[:, pl.ds(2 * units, WIDTH)]
    sums = [sum_up, sum_down] + ([sum_w, sum_gain] if last else [])

    def bring():
        return [pltpu.make_async_copy(carry[k], brought[k], sems.at[k]) for k in range(len(brought))]

    def load(at):
        side = pl.ds(at * units, WIDTH if at == 2 else units)
        return pltpu.make_async_copy(weights.at[0, :, side], held.at[:, side], loaded.at[at])

    @pl.when(step == 0)
    def _():
        for at in (2, 0, 1) if first else (0, 1):
            load(at).start()
        for copy in bring():
            copy.start()
        for total in sums:
            total[...] = jnp.zeros_like(total)
        if first:
            load(2).wait()
            w_out[...] = w_ref[...]

    if first or last:
        spread(turned, mixed, where[0])
    if first:
        hidden = x_ref[0].astype(f32) + times(turned[...].T, w_ref[...])
        hidden_out[...] = hidden
        scaled = (hidden * rms(hidden)).astype(bf16)
        scaled_out[...] = scaled
    else:
        scaled = scaled_ref[...]

    @pl.when(step == 0)
    def _():
        load(0).wait()
        load(1).wait()

    grad = grad_ref[0]
    slab = 256
    for k in range(units // slab):
        at = pl.ds(k * slab, slab)
        inner = pl.ds(k * slab % WIDTH, slab)
        pre = turned_by_rows(up_ref[:, at], scaled)
        grad_active = rows_by_rows(downs[k * slab // WIDTH][inner, :], grad)
        square = pre * pre
        half = 0.5 + 0.5 * jnp.tanh(pre * (FIRST + SECOND * square))
        act = pre * half
        active[at, :] = act.astype(bf16)
        slope = half + act * (1.0 - half) * (2.0 * FIRST + 6.0 * SECOND * square)
        grad_pre[at, :] = (grad_active * slope).astype(bf16)
    out = sum(
        turned_times(downs[q][...], active[pl.ds(q * WIDTH, WIDTH), :]) for q in range(slices)
    )
    back = times(up_ref[...], grad_pre[...])
    if not first:
        out, back = out + out_ref[...], back + back_ref[...]
    for q in range(slices):
        at = pl.ds(q * WIDTH, WIDTH)
        sum_down[at, :] += times(active[at, :], grad)
        sum_up[at, :] += times(grad_pre[at, :], scaled)
    if last:
        hidden = hidden if first else hidden_ref[...]
        result_ref[0] = (hidden + out.T).astype(bf16)
        weighted = back.T
        scale = rms(hidden)
        both = weighted * hidden
        mean = jnp.mean(both, axis=-1, keepdims=True)
        attended = (grad.astype(f32) + scale * weighted - hidden * (scale**3 * mean)).astype(bf16)
        grad_hidden_ref[...] = attended
        scratch[...] = rows_by_rows(w_ref[...], attended).astype(bf16)
        pick(scratch, grads, where[0])
        sum_w[...] += times(turned[...], attended)
        sum_gain[...] += jnp.sum(both * scale, axis=0, keepdims=True)
    else:
        out_next[...] = out
        back_next[...] = back

    @pl.when(final)
    def _():
        for copy in bring():
            copy.wait()
        for total, more in zip(sums, brought):
            total[...] += more[...].astype(f32)
        if settled:
            for q in range(slices):
                at = pl.ds(q * WIDTH, WIDTH)
                up_ref[:, at] = sum_up[at, :].T.astype(bf16)
                down_ref[:, at] = sum_down[at, :].astype(bf16)
            if last:
                halves(sum_w[...], sum_gain[...], low, high)
            if plain:
                joint[0][...] = held[:, pl.ds(0, 2 * units)]
                if last:
                    joint[1][:, pl.ds(0, low.shape[1])] = low[...]
                    joint[1][:, pl.ds(low.shape[1], low.shape[1])] = high[...]
            else:
                share_two(where[2], units_at, 0, keeps, sends, up_ref, down_ref)
                if last:
                    share_two(where[2], units_at, 0, w_keeps, w_sends, low, high)
        else:
            for total, ref in zip(sums, handed):
                ref[...] = total[...].astype(ref.dtype)


def feed(where, units_at, item, chunk, grad, packed, w_out, tokens, mixed, state, carry, earlier, shapes, settled, after=()):
    rows = 256
    groups, parts, plain = len(mixed), [len(kind) for kind in shapes or ()], shapes is None
    group = mixed[0].shape[0]
    first, last = chunk == 0, chunk == CHUNKS - 1
    slices = HIDDEN // CHUNKS // WIDTH
    units = slices * WIDTH
    once = pl.Buffered(1)
    tall = pl.BlockSpec((1, rows, WIDTH), lambda j, *_: (item, j, 0))
    flat = pl.BlockSpec((rows, WIDTH), lambda j, *_: (j, 0))
    wide = pl.BlockSpec((WIDTH, rows), lambda j, *_: (0, j))
    split = pl.BlockSpec((group, rows), lambda j, *_: (0, j))
    square = pl.BlockSpec((WIDTH, WIDTH), lambda j, *_: (0, 0), pipeline_mode=once)
    operands = [(grad, tall), (packed, ANY)]
    if first or last:
        operands += [(m, split) for m in mixed]
    if last and not first:
        operands += [(w_out, square)]
    if first:
        operands += [(tokens, tall)]
    else:
        operands += list(zip(state, (flat, flat, wide, wide)))
    aliases = {}
    if carry:
        operands += [(c, ANY) for c in carry]
    outputs = []
    if first:
        outputs += [(shape(LENGTH, WIDTH, kind=f32), flat), (shape(LENGTH, WIDTH), flat), (shape(WIDTH, WIDTH), square)]
    if last:
        if carry:
            aliases = {2 + len(operands): len(outputs)}
            operands += [(e, ANY) for e in earlier]
        outputs += [(shape(*grad.shape), tall), (shape(LENGTH, WIDTH), flat)]
        outputs += [(shape(group, LENGTH), split)] * groups
    else:
        outputs += [(shape(WIDTH, LENGTH, kind=f32), wide)] * 2
    fixed = len(outputs)
    handed = [shape(units, WIDTH)] * 2
    if last:
        handed += [shape(WIDTH, WIDTH), shape(1, WIDTH, kind=f32)]
    if settled:
        if plain:
            sizes = [shape(WIDTH, 2 * units), shape(WIDTH, WIDTH + 256)][: 1 + last]
        else:
            sizes = [shape(c, r, units) for kind in shapes for c, r in kind]
            if last:
                sizes += [shape(c, r, WIDTH // 2 + 128) for kind in shapes for c, r in kind]
        outputs += [
            (u, pl.BlockSpec(u.shape, lambda j, *_, n=len(u.shape): (0,) * n, pipeline_mode=once))
            for u in sizes
        ]
    else:
        sizes = handed
        outputs += [(u, pl.BlockSpec(u.shape, lambda j, *_: (0, 0), pipeline_mode=once)) for u in sizes]
    scratch = [
        pltpu.VMEM((WIDTH, 2 * units + WIDTH * first), bf16),
        pltpu.VMEM((units, rows), bf16),
        pltpu.VMEM((units, rows), bf16),
        pltpu.VMEM((units, WIDTH), f32),
        pltpu.VMEM((units, WIDTH), f32),
        pltpu.SemaphoreType.DMA((4,)),
        pltpu.SemaphoreType.DMA((3,)),
    ]
    if carry:
        scratch += [pltpu.VMEM(u.shape, u.dtype) for u in handed]
    if first or last:
        scratch += [pltpu.VMEM((WIDTH, rows), bf16)]
    if last:
        scratch += [
            pltpu.VMEM((WIDTH, rows), bf16),
            pltpu.VMEM((WIDTH, WIDTH), f32),
            pltpu.VMEM((1, WIDTH), f32),
            pltpu.VMEM((WIDTH, WIDTH // 2 + 128), bf16),
            pltpu.VMEM((WIDTH, WIDTH // 2 + 128), bf16),
        ]
    outs = call(
        functools.partial(
            feed_kernel,
            first=first,
            last=last,
            carried=bool(carry),
            settled=settled,
            plain=plain,
            slices=slices,
            groups=groups,
            parts=parts,
        ),
        "feed",
        (LENGTH // rows,),
        [where, units_at],
        operands,
        outputs,
        scratch,
        12 * LENGTH * WIDTH * units,
        20 << 20,
        after,
        aliases,
    )
    main, sums = outs[:fixed], outs[fixed:]
    if settled and not plain:
        keep, both = parts[0], sum(parts)
        sums = [(sums[at : at + keep], sums[at + keep : at + both]) for at in range(0, len(sums), both)]
    return main, sums


def tokens_kernel(where, units_at, *refs, groups, parts, carried, settled, plain):
    refs = Refs(refs)
    x_ref, grad_ref, w_ref, grads = refs.take(), refs.take(), refs.take(), refs.take(groups)
    if carried:
        carry = refs.take(2)
        refs.take()
    result_ref = refs.take()
    if settled and plain:
        joint = refs.take()
    elif settled:
        keeps, sends = refs.take(parts[0]), refs.take(parts[1])
    else:
        handed = refs.take(2)
    turned, sum_w, sum_gain, low, high, sems = refs.take(6)
    brought = refs.take(2) if carried else ()
    step = pl.program_id(0)
    sums = [sum_w, sum_gain]

    def bring():
        return [pltpu.make_async_copy(carry[k], brought[k], sems.at[k]) for k in range(2)] if carried else []

    @pl.when(step == 0)
    def _():
        for copy in bring():
            copy.start()
        for total in sums:
            total[...] = jnp.zeros_like(total)

    spread(turned, grads, where[0])
    x = x_ref[0].astype(f32)
    scale = rms(x)
    scaled = (x * scale).astype(bf16)
    weighted = rows_by_rows(turned[...].T, w_ref[...])
    both = weighted * x
    mean = jnp.mean(both, axis=-1, keepdims=True)
    total = grad_ref[...].astype(f32) + scale * weighted - x * (scale**3 * mean)
    result_ref[0] = total.astype(bf16)
    sum_gain[...] += jnp.sum(both * scale, axis=0, keepdims=True)
    sum_w[...] += times(turned[...], scaled)

    @pl.when(step == pl.num_programs(0) - 1)
    def _():
        for copy in bring():
            copy.wait()
        for total, more in zip(sums, brought):
            total[...] += more[...]
        if settled:
            halves(sum_w[...].T, sum_gain[...], low, high)
            if plain:
                joint[:, pl.ds(0, low.shape[1])] = low[...]
                joint[:, pl.ds(low.shape[1], low.shape[1])] = high[...]
            else:
                share_two(where[2], units_at, 0, keeps, sends, low, high)
        else:
            copies = [pltpu.make_async_copy(sums[k], handed[k], sems.at[k]) for k in range(2)]
            for copy in copies:
                copy.start()
            for copy in copies:
                copy.wait()


def grad_tokens_of(where, units_at, item, tokens, grad_hidden, weight, grads, carry, earlier, shapes, settled, after=()):
    rows = 256
    groups, parts, plain = len(grads), [len(kind) for kind in shapes or ()], shapes is None
    group = grads[0].shape[0]
    tall = pl.BlockSpec((1, rows, WIDTH), lambda j, *_: (item, j, 0))
    whole = lambda j, *_: (0, 0)
    operands = [
        (tokens, tall),
        (grad_hidden, pl.BlockSpec((rows, WIDTH), lambda j, *_: (j, 0))),
        (weight, pl.BlockSpec((WIDTH, WIDTH), whole)),
    ] + [(g, pl.BlockSpec((group, rows), lambda j, *_: (0, j))) for g in grads]
    aliases = {}
    if carry:
        operands += [(c, ANY) for c in carry]
        aliases = {2 + len(operands): 0}
        operands += [(earlier, ANY)]
    outputs = [(shape(*tokens.shape), tall)]
    half = WIDTH // 2 + 128
    if settled:
        sizes = [shape(c, r, half) for kind in shapes or () for c, r in kind]
        outputs += [(u, pl.BlockSpec(u.shape, lambda j, *_: (0, 0, 0))) for u in sizes]
        if plain:
            outputs += [(shape(WIDTH, 2 * half), pl.BlockSpec((WIDTH, 2 * half), whole))]
    else:
        outputs += [(shape(WIDTH, WIDTH, kind=f32), ANY), (shape(1, WIDTH, kind=f32), ANY)]
    outs = call(
        functools.partial(tokens_kernel, groups=groups, parts=parts, carried=bool(carry), settled=settled, plain=plain),
        "grad_tokens",
        (LENGTH // rows,),
        [where, units_at],
        operands,
        outputs,
        [
            pltpu.VMEM((WIDTH, rows), bf16),
            pltpu.VMEM((WIDTH, WIDTH), f32),
            pltpu.VMEM((1, WIDTH), f32),
            pltpu.VMEM((WIDTH, half), bf16),
            pltpu.VMEM((WIDTH, half), bf16),
            pltpu.SemaphoreType.DMA((2,)),
        ]
        + [pltpu.VMEM((WIDTH, WIDTH), f32), pltpu.VMEM((1, WIDTH), f32)][: 2 * bool(carry)],
        4 * LENGTH * WIDTH * WIDTH,
        8 << 20,
        after,
        aliases,
    )
    if settled and not plain:
        return outs[0], (outs[1 : 1 + parts[0]], outs[1 + parts[0] :])
    return outs[0], outs[1:]


def halved(array):
    half = array.shape[1] // 2
    return array[:, :half], array[:, half:]


def hold(*values):
    return lax.optimization_barrier(values)


def exchange(parts):
    got = [parts[0]]
    for r in range(1, len(parts)):
        got.append(lax.ppermute(parts[r], "dp", [(i, i ^ r) for i in range(len(parts))]))
    return got


def add(*terms):
    return functools.reduce(jnp.add, [t.astype(f32) for t in terms]).astype(bf16)


class Chips:
    def __init__(self, groups, seqs):
        self.groups, self.seqs, self.rings = groups, seqs, seqs // 2
        self.here, self.row = lax.axis_index("dp"), lax.axis_index("seq")
        self.core, self.z = self.row % 2, self.row // 2

    def across(self, array):
        return lax.ppermute(array, "seq", [(i, i ^ 1) for i in range(self.seqs)])

    def along(self, array, step):
        n = self.seqs
        return lax.ppermute(array, "seq", [(i, (i + 2 * step) % n) for i in range(n)])

    def over(self, array, bits):
        return lax.ppermute(array, "dp", [(i, i ^ bits) for i in range(self.groups)])

    def hop(self, array, step):
        return lax.ppermute(array, "seq", [(i, i ^ (2 * step)) for i in range(self.seqs)])

    def chip(self, bits, step):
        return (self.here ^ bits) * self.rings + (self.z ^ step)

    def chips(self):
        return [self.chip(b, s) for b in range(self.groups) for s in range(self.rings)]

    def gather_line(self, mine):
        return jnp.stack([mine] + [self.hop(mine, s) for s in range(1, self.rings)])

    def gather_plane(self, ring):
        return [ring] + [self.over(ring, bits) for bits in range(1, self.groups)]

    def gathered_at(self, rows):
        return jnp.stack([v for c in self.chips() for v in (c * rows, 0 * c)]).astype(jnp.int32)

    def unit_order(self, rows):
        return jnp.stack([c * rows for c in self.chips()]).astype(jnp.int32)

    def scatter_core(self, shares):
        return self.join_core(shares[0], self.across(shares[1][0]))

    def join_core(self, keeps, got):
        n = self.rings
        return [add(keep, got[b * n : (b + 1) * n]) for b, keep in enumerate(keeps)]

    def scatter_plane(self, parts):
        return self.join_plane([parts[0]] + [self.over(parts[b], b) for b in range(1, self.groups)])

    def join_plane(self, parts):
        return [add(*[part[s] for part in parts]) for s in range(self.rings)]

    def scatter_line(self, own):
        return add(own[0], *[self.hop(own[s], s) for s in range(1, self.rings)])

    def settle(self, total):
        rows = total.shape[0] // 2
        mine = lax.dynamic_slice_in_dim(total, self.core * rows, rows)
        other = self.across(lax.dynamic_slice_in_dim(total, (1 - self.core) * rows, rows))
        first = self.core == 0
        return jnp.where(first, mine, other), jnp.where(first, other, mine)


def body(tokens, lengths, mixer, gain_one, gain_two, w_value, w_out, w_up, w_down, cotangent, groups, seqs):
    ranks = groups * seqs
    fast = groups == 4 and seqs == 8
    chips = Chips(groups, seqs)
    here, row, core = chips.here, chips.row, chips.core
    where = jnp.stack([here, row, core]).astype(jnp.int32)
    items = tokens.shape[0]
    shard = w_value.shape[0]
    slices = HIDDEN // WIDTH
    width = slices // CHUNKS
    half = WIDTH // 2

    first_gain = gain_one.astype(f32)[:, None]
    second_gain = gain_two.astype(f32)[:, None]
    value_mine = (w_value.astype(f32) * first_gain).astype(bf16)
    if fast:
        other = chips.across(value_mine)
        value_unit = jnp.where(
            core == 0, jnp.concatenate([value_mine, other]), jnp.concatenate([other, value_mine])
        )
        value_unit, lengths_here, w_up, w_down, w_out, mixer = hold(
            value_unit, jnp.stack(exchange([lengths] * groups), axis=1).reshape(-1), w_up, w_down, w_out, mixer
        )
    up_mine = (w_up.astype(f32) * second_gain).astype(bf16)
    up_mine = up_mine.reshape(shard, ranks, slices, shard).swapaxes(1, 2)
    down_mine = w_down.reshape(slices, shard, WIDTH).swapaxes(0, 1)
    weights = [value_mine]
    for chunk in range(CHUNKS):
        at = slice(chunk * width, (chunk + 1) * width)
        columns = [m[:, at].reshape(shard, width * WIDTH) for m in (up_mine, down_mine)]
        weights.append(jnp.concatenate(columns + [w_out][chunk:], axis=1))

    logits = jnp.exp(mixer.astype(f32))
    logits_low = logits.astype(bf16)
    block = logits.shape[1]
    shares_at, shares = [0], ((1, LENGTH),)
    early = weights[1:2] if fast else weights
    whole = [lax.all_gather(w, ALL, axis=0, tiled=True)[None] for w in early]
    weights_at = [jnp.zeros((2,), jnp.int32)] * (1 + CHUNKS)
    if fast:
        rings = chips.rings
        whole = [None] + whole
        weights_at[0] = chips.gathered_at(2 * shard)
        zs = [(chips.z - s) % rings for s in (0, 1, 3, 2)]
        logits_at = [(2 * z + c) * block for c in (core, 1 - core) for z in zs]
        shapes = (((rings, 2 * shard),) * groups, ((groups * rings, 2 * shard),))
        order = chips.unit_order(2 * shard)
    else:
        value_parts = whole[:1]
        logits_parts = [lax.all_gather(logits_low, "seq", axis=1, tiled=True)]
        logits_at = [0]
        shapes = None
        order = jnp.zeros((1,), jnp.int32)
    logits_at, shares_at = (
        jnp.stack([jnp.asarray(v, jnp.int32) for v in at]) for at in (logits_at, shares_at)
    )
    def fed(pairs):
        ups, downs = (jnp.concatenate(parts, axis=1).astype(f32) for parts in zip(*pairs))
        sum_up = ups.reshape(shard, slices, ranks, shard).swapaxes(1, 2).reshape(shard, HIDDEN)
        sum_down = downs.reshape(shard, slices, WIDTH).swapaxes(0, 1)
        return sum_up * second_gain, sum_down.reshape(shard * slices, WIDTH)

    def joined(pair):
        low, high = (part.astype(f32) for part in pair)
        return jnp.concatenate([low[:, :half], high[:, :half]], axis=1), low[:, half] + high[:, half]

    def lengths_of():
        return jnp.stack(exchange([lengths] * groups), axis=1).reshape(-1)

    def values_of(after=()):
        return project_values(where, weights_at[0], tokens, value_parts, groups, after)

    def mix(item, values, after=()):
        return mix_items(lengths_here, logits_at, values, logits_parts, item, after)

    def run_feed(item, chunk, packed, w_out_all, mixed, state, carry, result, after=()):
        return feed(
            where, order, item, chunk, cotangent, packed, w_out_all, tokens,
            mixed, state, carry, (result,), shapes if chunk else None, item == items - 1, after,
        )

    def back(item, grads, mixed_out, sums, after=()):
        return values_back(
            lengths_here, logits_at, grads, mixed_out, sums, logits_parts, item * groups, after
        )

    def close(item, grad_hidden, grads, carry, earlier, after=()):
        return grad_tokens_of(
            where, order, item, tokens, grad_hidden, value_all, grads, carry, earlier, shapes,
            item == items - 1, after,
        )

    if fast:
        assert items == 2 and CHUNKS == 2
        value_ring = chips.gather_line(value_unit)
        value_ring, logits_low, second = hold(value_ring, logits_low, weights[2])
        value_parts = chips.gather_plane(value_ring)
        next_one, last_one = chips.along(logits_low, 1), chips.along(logits_low, 3)
        values, value_all = values_of()
        values = exchange(values)
        next_two = chips.along(next_one, 1)
        values, logits_low = hold(values, logits_low)
        next_two, last_one, values = hold(next_two, last_one, values)
        logits_parts = [logits_low, next_one, last_one, next_two]
        logits_parts += [chips.across(r) for r in logits_parts]
        mixed_out_a, sums_a = mix(0, values)
        mixed_out_a, sums_a, second = hold(mixed_out_a, sums_a, second)
        second = lax.all_gather(second, ALL, axis=0, tiled=True)
        mixed_a = exchange(mixed_out_a)
        mixed_out_b, sums_b = mix(1, values)
        mixed_out_b, mixed_a = hold(mixed_out_b, mixed_a)
        mixed_b = exchange(mixed_out_b)
        first = whole[1]
        state_a, carry = run_feed(0, 0, first, None, mixed_a, None, (), None)
        state_a, carry, mixed_b = hold(state_a, carry, mixed_b)
        w_out_all = state_a[2]
        state_b, (shared,) = run_feed(1, 0, first, None, mixed_b, None, carry, None)
        first_sums = lax.psum_scatter(shared, ALL, scatter_dimension=0, tiled=True)
        state_a = state_a[:2] + state_a[3:]
        state_b = state_b[:2] + state_b[3:]
        second = second[None]
        out_a, carry = run_feed(0, 1, second, w_out_all, mixed_a, state_a, (), None)
        out_a, carry = hold(out_a, carry)
        grads_a = exchange(out_a[2:])
        out_b, (second_shared, out_shared) = run_feed(
            1, 1, second, w_out_all, mixed_b, state_b, carry, out_a[0]
        )
        out_b, grads_a, second_shared, out_shared = hold(out_b, grads_a, second_shared, out_shared)
        result = out_b[0]
        grads_b = exchange(out_b[2:])
        back_a, left_a = back(0, grads_a, mixed_out_a, sums_a)
        back_a, left_a, second_shared, out_shared = hold(back_a, left_a, second_shared, out_shared)
        back_a = exchange(back_a)
        back_b, left_b = back(1, grads_b, mixed_out_b, sums_b)
        back_b, left_b, second_shared, out_shared = hold(back_b, left_b, second_shared, out_shared)
        back_b = exchange(back_b)
        grad_logits = logits_back(lengths_here, shares_at, [left_a, left_b], values, shares)
        grad_logits, back_a, second_shared, out_shared = hold(
            grad_logits, back_a, second_shared, out_shared
        )
        grad_mixer = lax.psum_scatter(grad_logits[0][0], "seq", scatter_dimension=1, tiled=True)
        second_got, out_got = chips.across(second_shared[1][0]), chips.across(out_shared[1][0])
        grad_tokens, carry = close(0, out_a[1], back_a, (), None)
        carry, back_b, grad_tokens, second_got, out_got = hold(
            carry, back_b, grad_tokens, second_got, out_got
        )
        second_sums = [
            jnp.concatenate(pair, axis=2)
            for pair in zip(chips.join_core(second_shared[0], second_got), chips.join_core(out_shared[0], out_got))
        ]
        second_plane = [chips.over(second_sums[b], b) for b in range(1, groups)]
        grad_tokens, shared = close(1, out_b[1], back_b, carry, grad_tokens)
        shared, second_plane[:2] = hold(shared, second_plane[:2])
        value_sums = chips.scatter_core(shared)
        value_sums, second_plane[2:] = hold(value_sums, second_plane[2:])
        second_sums = chips.join_plane([second_sums[0]] + list(second_plane))
        second_line = [chips.hop(second_sums[k], k) for k in range(1, rings)]
        value_sums = chips.scatter_plane(value_sums)
        value_sums, second_line = hold(value_sums, second_line)
        value_line = [chips.hop(value_sums[k], k) for k in range(1, rings)]
        second_sums = chips.settle(add(second_sums[0], *second_line))
        wide = width * WIDTH
        sum_up, sum_down = fed([halved(first_sums), tuple(part[:, :wide] for part in second_sums)])
        sum_out, gain_two_sum = joined([part[:, wide:] for part in second_sums])
        grad_mixer = grad_mixer.astype(f32) * logits
        value_line, grad_mixer, sum_up, sum_down, sum_out, gain_two_sum = hold(
            value_line, grad_mixer, sum_up, sum_down, sum_out, gain_two_sum
        )
        settled = [chips.settle(add(value_sums[0], *value_line))]
    else:
        lengths_here = lengths_of()
        values, value_all = values_of()
        values = exchange(values)
        mixed_out, sums, mixed = [], [], []
        for item in range(items):
            out, total = mix(item, values)
            mixed_out.append(out)
            sums.append(total)
            mixed.append(exchange(out))
        states, w_out_all, result = [None] * items, None, None
        grads, grad_hidden, shared = [None] * items, [None] * items, []
        for chunk in range(CHUNKS):
            carry = ()
            for item in range(items):
                state, carry = run_feed(
                    item, chunk, whole[1 + chunk], w_out_all, mixed[item], states[item], carry, result
                )
                if chunk == CHUNKS - 1:
                    result, grad_hidden[item], grads[item] = state[0], state[1], exchange(state[2:])
                elif chunk == 0:
                    if item == items - 1:
                        w_out_all = state[2]
                    states[item] = list(state[:2]) + list(state[3:])
                else:
                    states[item] = list(states[item][:2]) + list(state)
            shared += carry
        lefts, grad_values = [], []
        for item in range(items):
            out, left = back(item, grads[item], mixed_out[item], sums[item])
            lefts.append(left)
            grad_values.append(exchange(out))
        grad_logits = logits_back(lengths_here, shares_at, lefts, values, shares)
        carry, grad_tokens = (), None
        for item in range(items):
            grad_tokens, carry = close(item, grad_hidden[item], grad_values[item], carry, grad_tokens)
        shared += carry
        grad_mixer = lax.psum_scatter(grad_logits[0][0], "seq", scatter_dimension=1, tiled=True)
        settled = [halved(lax.psum_scatter(x, ALL, scatter_dimension=0, tiled=True)) for x in shared]
    if not fast:
        sum_up, sum_down = fed(settled[:CHUNKS])
        sum_out, gain_two_sum = joined(settled[CHUNKS])
        grad_mixer = grad_mixer.astype(f32) * logits
    sum_value, gain_one_sum = joined(settled[-1])
    return (
        result,
        grad_tokens,
        grad_mixer,
        gain_one_sum / first_gain[:, 0],
        gain_two_sum / second_gain[:, 0],
        sum_value * first_gain,
        sum_out,
        sum_up,
        sum_down,
    )


def solution(mesh):
    rows = P(ALL, None)
    line = P(ALL)
    cube = P(ALL, None, None)
    logits = P("dp", "seq", None)
    return jax.shard_map(
        functools.partial(body, groups=mesh.shape["dp"], seqs=mesh.shape["seq"]),
        mesh=mesh,
        in_specs=(cube, line, logits, line, line, rows, rows, rows, rows, cube),
        out_specs=(cube, cube, logits, line, line, rows, rows, rows, rows),
        check_vma=False,
    )
```
